32 devices in a mesh: dom: 16 (over z, y, x), hid: 2 (over core).
Axes of the slice: x: 2, y: 2, z: 4, core: 2. Of those that a mesh axis runs over, the one named last changes fastest.
Arguments:
- features: bfloat16 [16384, 512], P('dom', 'hid'), may hold values from -6 to 6
- history: bfloat16 [16384, 512], P('dom', 'hid'), may hold values from -6 to 6
- remote_tiles: bfloat16 [16, 16, 128, 128], P('dom'), may hold values from -0.21875 to 0.21875
- remote_dst: int32 [16, 16], P('dom'), may hold values from 0 to 7
- serve_block: int32 [16, 16], P('dom'), may hold values from 0 to 7
- push_flag: int32 [16, 16], P('dom'), may hold values 0 or 1
- local_tiles: bfloat16 [16, 32, 128, 128], P('dom'), may hold values from -0.21875 to 0.21875
- local_src: int32 [16, 32], P('dom'), may hold values from 0 to 7
- local_dst: int32 [16, 32], P('dom'), may hold values from 0 to 7
- weight_in: bfloat16 [512, 512], P('hid'), may hold values from -0.25 to 0.25
- weight_out: bfloat16 [512, 512], P('hid'), may hold values from -0.25 to 0.25
- cotangent: bfloat16 [16384, 512], P('dom', 'hid'), may hold values from -6 to 6
Outputs:
- out: bfloat16 [16384, 512], P('dom', 'hid')
- grad_hidden: bfloat16 [16384, 512], P('dom', 'hid')
- grad_weight_in: float32 [512, 512], P('hid')
- grad_weight_out: float32 [512, 512], P('hid')
The draws below stay inside these ranges and needn't reach their ends.
Inputs may be any that keep to these rules, and one draw needn't show every extreme that they name: `remote_dst`: local block indices. `serve_block`: local block indices. `local_src`: local block indices. `local_dst`: local block indices.
All inputs are finite; a program needn't handle non-finite values. No bound on the sum of `push_flag` on one device may be relied on, other than what follows from the above.
Results may differ from the reference program's by a relative error of at most 0.007.
Values may be sent and summed in bfloat16 or wider, within the bound.
No kernel may reach another device: no remote copies, remote signals or barrier semaphores. Data moves between devices by JAX's collectives and lax.ppermute only.
A program may use at most 128 MiB of HBM per device.

```python
import math
import jax
import jax.numpy as jnp
from jax import lax

F = 512
TILE = 128
NB = 8
LOC = 32
NPART = 16
NODES = 16384


def touch_ends(entries, stream_key, smallest, top_value):
    shape = entries.shape
    place = [jax.random.randint(jax.random.fold_in(stream_key, axis), (), 0, shape[axis]) for axis in range(len(shape))]
    entries = entries.at[tuple(place)].set(smallest)
    longest = shape.index(max(shape))
    place[longest] = (place[longest] + 1) % shape[longest]
    return entries.at[tuple(place)].set(top_value)


def block_levels(key, extent, split, low, high):
    gain, own = 1.0, jax.random.fold_in(key, 6)
    for dim, shards_of in split:
        steps = jnp.exp(jax.random.uniform(jax.random.fold_in(own, dim), (shards_of,), jnp.float32, low / len(split), high / len(split)))
        gain = gain * jnp.repeat(steps, extent[dim] // shards_of).reshape([-1 if axis == dim else 1 for axis in range(len(extent))])
    return gain


def normal_values(key, dims, width, bound, shards=(), held_as=jnp.bfloat16):
    result = width * jax.random.normal(key, dims, jnp.float32)
    if shards:
        result = result * block_levels(key, dims, shards, -0.22, 0.18)
    return jnp.clip(result, -bound, bound).astype(held_as)


def setup_inputs(seed: int = 0) -> dict:
    streams_of = jax.random.split(jax.random.key(seed), 13)
    return {
        "features": normal_values(streams_of[0], (NODES, F), 1.0, 6.0, ((0, 16), (1, 2))),
        "history": normal_values(streams_of[1], (NODES, F), 1.0, 6.0, ((0, 16), (1, 2))),
        "remote_tiles": normal_values(streams_of[2], (NPART, NPART, TILE, TILE), (TILE * (NPART + LOC) // NB) ** -0.5, 0.21875, ((0, 16),)),
        "remote_dst": touch_ends(jax.random.randint(streams_of[3], (NPART, NPART), 0, NB), jax.random.fold_in(streams_of[3], 1), 0, NB - 1).astype(jnp.int32),
        "serve_block": touch_ends(jax.random.randint(streams_of[4], (NPART, NPART), 0, NB), jax.random.fold_in(streams_of[4], 1), 0, NB - 1).astype(jnp.int32),
        "push_flag": touch_ends((jax.random.randint(streams_of[5], (NPART, NPART), 0, 2) < 1).astype(jnp.int32), jax.random.fold_in(streams_of[5], 1), 0, 1),
        "local_tiles": normal_values(streams_of[6], (NPART, LOC, TILE, TILE), (TILE * (NPART + LOC) // NB) ** -0.5, 0.21875, ((0, 16),)),
        "local_src": touch_ends(jax.random.randint(streams_of[7], (NPART, LOC), 0, NB), jax.random.fold_in(streams_of[7], 1), 0, NB - 1).astype(jnp.int32),
        "local_dst": touch_ends(jax.random.randint(streams_of[8], (NPART, LOC), 0, NB), jax.random.fold_in(streams_of[8], 1), 0, NB - 1).astype(jnp.int32),
        "weight_in": normal_values(streams_of[9], (F, F), F ** -0.5, 0.25, ((0, 2),)),
        "weight_out": normal_values(streams_of[10], (F, F), F ** -0.5, 0.25, ((0, 2),)),
        "cotangent": normal_values(streams_of[11], (NODES, F), 1.0, 6.0, ((0, 16), (1, 2))),
    }


def reference(features, history, remote_tiles, remote_dst, serve_block, push_flag, local_tiles, local_src, local_dst, weight_in, weight_out, cotangent):
    nodes = NPART * NB * TILE
    parts = jnp.arange(NPART, dtype=jnp.int32)
    blocks_ids = jnp.arange(NB, dtype=jnp.int32)
    highest = lax.Precision.HIGHEST

    def blocks(values):
        return values.reshape(NPART, NB, TILE, F)

    def aggregate(node_blocks, supply):

        def single(part):
            rows = node_blocks[part][local_src[part]]
            inner = jnp.einsum('kij,kjf->kif', local_tiles[part].astype(jnp.float32), rows.astype(jnp.float32), precision=highest)
            hot_local = (local_dst[part][:, None] == blocks_ids).astype(jnp.float32)
            total = jnp.einsum('kb,kif->bif', hot_local, inner, precision=highest)
            outer = jnp.einsum('qij,qjf->qif', remote_tiles[part].astype(jnp.float32), supply(part).astype(jnp.float32), precision=highest)
            hot_remote = (remote_dst[part][:, None] == blocks_ids).astype(jnp.float32)
            total = total + jnp.einsum('qb,qif->bif', hot_remote, outer, precision=highest)
            return total.reshape(NB * TILE, F)
        return lax.map(single, parts).reshape(nodes, F).astype(jnp.bfloat16)
    feat_blocks = blocks(features)
    z_first = aggregate(feat_blocks, lambda part: feat_blocks[parts, serve_block[:, part]])
    pre_first = jnp.dot(z_first, weight_in, preferred_element_type=jnp.float32)
    hidden = jax.nn.silu(pre_first).astype(jnp.bfloat16)
    hidden_blocks = blocks(hidden)
    hist_blocks = blocks(history)

    def served(part):
        chosen = serve_block[:, part]
        return jnp.where((push_flag[:, part] == 1)[:, None, None], hidden_blocks[parts, chosen], hist_blocks[parts, chosen])
    z_second = aggregate(hidden_blocks, served)
    out = jnp.dot(z_second, weight_out, preferred_element_type=jnp.float32).astype(jnp.bfloat16)
    grad_z = jnp.dot(cotangent, weight_out.T, preferred_element_type=jnp.float32).astype(jnp.bfloat16)
    grad_blocks = blocks(grad_z)

    def back_step(accum, part):
        inner = jnp.einsum('kji,kjf->kif', local_tiles[part].astype(jnp.float32), grad_blocks[part][local_dst[part]].astype(jnp.float32), precision=highest)
        hot_local = (local_src[part][:, None] == blocks_ids).astype(jnp.float32)
        accum = accum.at[part].add(jnp.einsum('kb,kif->bif', hot_local, inner, precision=highest))
        outer = jnp.einsum('qji,qjf->qif', remote_tiles[part].astype(jnp.float32), grad_blocks[part][remote_dst[part]].astype(jnp.float32), precision=highest).astype(jnp.bfloat16)
        flags = push_flag[:, part].astype(jnp.float32)[:, None, None]
        accum = accum.at[parts, serve_block[:, part]].add(flags * outer.astype(jnp.float32))
        return (accum, None)
    grad_acc, _ = lax.scan(back_step, jnp.zeros((NPART, NB, TILE, F), jnp.float32), parts)
    grad_acc = grad_acc.reshape(nodes, F)
    sig = jax.nn.sigmoid(pre_first)
    grad_pre = (grad_acc * sig * (1.0 + pre_first * (1.0 - sig))).astype(jnp.bfloat16)
    scale = 1.0 / math.sqrt(nodes)
    grad_weight_in = jnp.dot(z_first.T, grad_pre, preferred_element_type=jnp.float32) * scale
    grad_weight_out = jnp.dot(z_second.T, cotangent, preferred_element_type=jnp.float32) * scale
    return (out, grad_acc.astype(jnp.bfloat16), grad_weight_in, grad_weight_out)
```

```python
import functools

import jax
import jax.numpy as jnp
from jax import lax
from jax.experimental import pallas as pl
from jax.experimental.pallas import tpu as pltpu
from jax.sharding import PartitionSpec as P

BF16 = jnp.bfloat16
F32 = jnp.float32
VMEM_BYTES = 40 * 1024 * 1024
SWAP = ((0, 1), (1, 0))


def dot(a, b):
    return jnp.dot(a, b, preferred_element_type=F32)


def dot_t(a, b):
    return lax.dot_general(a, b, (((0,), (0,)), ((), ())), preferred_element_type=F32)


def dot_nt(a, b):
    return lax.dot_general(a, b, (((1,), (1,)), ((), ())), preferred_element_type=F32)


def call(body, scalars, arrays, grid, in_specs, out_specs, out_shape, scratch=(), flops=0, name=None):
    moved = sum(a.size * a.dtype.itemsize for a in arrays)
    moved += sum(s.size * s.dtype.itemsize for s in jax.tree.leaves(out_shape))
    return pl.pallas_call(
        body,
        grid_spec=pltpu.PrefetchScalarGridSpec(
            num_scalar_prefetch=len(scalars),
            grid=grid,
            in_specs=in_specs,
            out_specs=out_specs,
            scratch_shapes=list(scratch),
        ),
        out_shape=out_shape,
        compiler_params=pltpu.CompilerParams(vmem_limit_bytes=VMEM_BYTES),
        cost_estimate=pl.CostEstimate(flops=int(flops), bytes_accessed=int(moved), transcendentals=0),
        name=name,
    )(*scalars, *arrays)


def whole(shape):
    return pl.BlockSpec(shape, lambda i, *_: (0,) * len(shape))


def lead(shape):
    return pl.BlockSpec(shape, lambda i, *_: (i,) + (0,) * (len(shape) - 1))


def group_of(peers):
    return 8 if peers % 8 == 0 else 1


def pick_blocks(ids, node_blocks):
    peers = ids.shape[0]
    _, tile, width = node_blocks.shape
    group = group_of(peers)

    def body(ids_ref, nodes_ref, out_ref):
        step = pl.program_id(0)
        for j in range(group):
            out_ref[j] = nodes_ref[ids_ref[step * group + j]]

    return call(
        body, (ids,), (node_blocks,), (peers // group,),
        [whole(node_blocks.shape)], lead((group, tile, width)),
        jax.ShapeDtypeStruct((peers, tile, width), node_blocks.dtype), name="pick_blocks",
    )


def remote_back(targets, tiles, grads):
    peers, tile, _ = tiles.shape
    width = grads.shape[2]
    group = group_of(peers)

    def body(ids_ref, tiles_ref, grads_ref, out_ref):
        step = pl.program_id(0)
        for j in range(group):
            out_ref[j] = dot_t(tiles_ref[j], grads_ref[ids_ref[step * group + j]]).astype(BF16)

    return call(
        body, (targets,), (tiles, grads), (peers // group,),
        [lead((group, tile, tile)), whole(grads.shape)], lead((group, tile, width)),
        jax.ShapeDtypeStruct((peers, tile, width), BF16),
        flops=2 * peers * tile * tile * width, name="remote_back",
    )


def local_both(sources, targets, tiles, nodes, grads):
    many, tile, _ = tiles.shape
    group = group_of(many)

    def body(src_ref, dst_ref, tiles_ref, nodes_ref, grads_ref, fwd_ref, bwd_ref):
        step = pl.program_id(0)

        @pl.when(step == 0)
        def _():
            fwd_ref[...] = jnp.zeros_like(fwd_ref)
            bwd_ref[...] = jnp.zeros_like(bwd_ref)

        for j in range(group):
            src = src_ref[step * group + j]
            dst = dst_ref[step * group + j]
            fwd_ref[dst] += dot(tiles_ref[j], nodes_ref[src])
            bwd_ref[src] += dot_t(tiles_ref[j], grads_ref[dst])

    shape = jax.ShapeDtypeStruct(nodes.shape, F32)
    return call(
        body, (sources, targets), (tiles, nodes, grads), (many // group,),
        [lead((group, tile, tile)), whole(nodes.shape), whole(grads.shape)],
        [whole(nodes.shape)] * 2, [shape, shape],
        flops=4 * many * tile * tile * nodes.shape[2], name="local_both",
    )


def local_forward(sources, targets, tiles, nodes):
    many, tile, _ = tiles.shape
    group = group_of(many)

    def body(src_ref, dst_ref, tiles_ref, nodes_ref, fwd_ref):
        step = pl.program_id(0)

        @pl.when(step == 0)
        def _():
            fwd_ref[...] = jnp.zeros_like(fwd_ref)

        for j in range(group):
            src = src_ref[step * group + j]
            dst = dst_ref[step * group + j]
            fwd_ref[dst] += dot(tiles_ref[j], nodes_ref[src])

    return call(
        body, (sources, targets), (tiles, nodes), (many // group,),
        [lead((group, tile, tile)), whole(nodes.shape)],
        whole(nodes.shape), jax.ShapeDtypeStruct(nodes.shape, F32),
        flops=2 * many * tile * tile * nodes.shape[2], name="local_forward",
    )


def remote_forward(targets, tiles, received, base):
    peers, tile, _ = tiles.shape
    width = received.shape[2]
    group = group_of(peers)
    steps = peers // group

    def body(dst_ref, tiles_ref, recv_ref, base_ref, out_ref, acc_ref):
        step = pl.program_id(0)

        @pl.when(step == 0)
        def _():
            acc_ref[...] = base_ref[...]

        for j in range(group):
            acc_ref[dst_ref[step * group + j]] += dot(tiles_ref[j], recv_ref[j])

        @pl.when(step == steps - 1)
        def _():
            out_ref[...] = acc_ref[...].astype(BF16)

    return call(
        body, (targets,), (tiles, received, base), (steps,),
        [lead((group, tile, tile)), lead((group, tile, width)), whole(base.shape)],
        whole(base.shape), jax.ShapeDtypeStruct(base.shape, BF16),
        [pltpu.VMEM(base.shape, F32)],
        flops=2 * peers * tile * tile * width, name="remote_forward",
    )


def middle(ids, flags, z_mine, z_other, w_in, w_out, hist_out):
    rows, half = z_mine.shape
    peers = ids.shape[0]
    count, tile, _ = hist_out.shape
    per = 2 if count % 2 == 0 else 1
    steps = count // per
    span = per * tile

    def body(ids_ref, flag_ref, zm_ref, zo_ref, wi_ref, wo_ref, hw_ref, pre_ref, hid_ref, prod_ref, send_ref):
        step = pl.program_id(0)
        pre = dot(zm_ref[...], wi_ref[:half]) + dot(zo_ref[...], wi_ref[half:])
        pre_ref[...] = pre
        hidden = (pre * (1.0 / (1.0 + jnp.exp(-pre)))).astype(BF16)
        hid_ref[...] = hidden
        prod = dot(hidden, wo_ref[:, :half]).astype(BF16)
        for j in range(per):
            prod_ref[step * per + j] = prod[j * tile : (j + 1) * tile]

        @pl.when(step == steps - 1)
        def _():
            for p in range(peers):
                fresh = flag_ref[p] == 1
                block = ids_ref[p]

                @pl.when(fresh)
                def _():
                    send_ref[p] = prod_ref[block]

                @pl.when(jnp.logical_not(fresh))
                def _():
                    send_ref[p] = hw_ref[block]

    return call(
        body, (ids, flags), (z_mine, z_other, w_in, w_out, hist_out), (steps,),
        [lead((span, half)), lead((span, half)), whole(w_in.shape), whole(w_out.shape), whole(hist_out.shape)],
        [lead((span, 2 * half)), lead((span, 2 * half)), whole(hist_out.shape), whole((peers, tile, half))],
        [
            jax.ShapeDtypeStruct((rows, 2 * half), F32),
            jax.ShapeDtypeStruct((rows, 2 * half), BF16),
            jax.ShapeDtypeStruct(hist_out.shape, BF16),
            jax.ShapeDtypeStruct((peers, tile, half), BF16),
        ],
        flops=12 * rows * half * half, name="middle",
    )


def gather_grads(ids, flags, returned, base):
    peers, tile, width = returned.shape
    count = base.shape[0]
    group = group_of(peers)
    steps = peers // group

    def body(ids_ref, flag_ref, ret_ref, base_ref, out_ref, acc_ref):
        step = pl.program_id(0)

        @pl.when(step == 0)
        def _():
            acc_ref[0] = base_ref[...]
            acc_ref[1] = jnp.zeros_like(base_ref)

        for j in range(group):
            p = step * group + j
            side = jnp.where(flag_ref[p] == 1, 0, 1)
            acc_ref[side, ids_ref[p]] += ret_ref[j].astype(F32)

        @pl.when(step == steps - 1)
        def _():
            out_ref[...] = acc_ref[...].astype(BF16)

    both = (2,) + base.shape
    return call(
        body, (ids, flags), (returned, base), (steps,),
        [lead((group, tile, width)), whole(base.shape)],
        whole(both), jax.ShapeDtypeStruct(both, BF16),
        [pltpu.VMEM(both, F32)], name="gather_grads",
    )


def chunking(peers, total, width):
    row_chunks = min(peers, total // 16)
    col_chunks = peers // row_chunks
    return row_chunks, col_chunks, total // row_chunks, width // col_chunks


def backward(place, sums_mine, sums_other, hidden, history, z_mine, pre, w_out, peers):
    _, rows, half = sums_mine.shape
    step_rows = rows // 4
    row_chunks, col_chunks, chunk_rows, chunk_cols = chunking(peers, 2 * half, 2 * half)

    def body(place_ref, sm_ref, so_ref, hid_ref, hist_ref, z_ref, pre_ref, wo_ref, gh_ref, chunk_ref, acc_ref):
        step = pl.program_id(0)
        me, side = place_ref[0], place_ref[1]

        @pl.when(step == 0)
        def _():
            acc_ref[...] = jnp.zeros_like(acc_ref)

        dh = dot_nt(sm_ref[0], wo_ref[:, :half]) + dot_nt(so_ref[0], wo_ref[:, half:])
        gh_ref[...] = dh[:, :half].astype(BF16)
        pre = pre_ref[...]
        s = 1.0 / (1.0 + jnp.exp(-pre))
        dpre = (dh * s * (1.0 + pre * (1.0 - s))).astype(BF16)
        z = z_ref[...]
        own = pl.ds(pl.multiple_of(side * half, half), half)
        far = pl.ds(pl.multiple_of((1 - side) * half, half), half)
        acc_ref[:half, own] += dot_t(z, dpre[:, :half])
        acc_ref[:half, far] += dot_t(z, dpre[:, half:])
        hid, hist = hid_ref[...], hist_ref[...]
        acc_ref[half:, own] += dot_t(hid, sm_ref[0]) + dot_t(hist, sm_ref[1])
        acc_ref[half:, far] += dot_t(hid, so_ref[0]) + dot_t(hist, so_ref[1])

        @pl.when(step == 3)
        def _():
            for c in range(peers):
                r, k = c // col_chunks, c % col_chunks
                piece = acc_ref[r * chunk_rows : (r + 1) * chunk_rows, k * chunk_cols : (k + 1) * chunk_cols]
                chunk_ref[c ^ me] = piece.astype(BF16)

    sums_spec = pl.BlockSpec((2, step_rows, half), lambda i, *_: (0, i, 0))
    return call(
        body, (place,), (sums_mine, sums_other, hidden, history, z_mine, pre, w_out), (4,),
        [
            sums_spec, sums_spec, lead((step_rows, half)), lead((step_rows, half)),
            lead((step_rows, half)), lead((step_rows, 2 * half)), whole(w_out.shape),
        ],
        [lead((step_rows, half)), whole((peers, chunk_rows, chunk_cols))],
        [
            jax.ShapeDtypeStruct((rows, half), BF16),
            jax.ShapeDtypeStruct((peers, chunk_rows, chunk_cols), BF16),
        ],
        [pltpu.VMEM((2 * half, 2 * half), F32)],
        flops=20 * rows * half * half, name="backward",
    )


def finish_weights(place, chunks, half, scale):
    peers, chunk_rows, chunk_cols = chunks.shape
    _, col_chunks, _, _ = chunking(peers, 2 * half, 2 * half)

    def body(place_ref, chunk_ref, in_ref, out_ref):
        me = place_ref[0]
        for c in range(peers):
            r, k = (c // col_chunks) * chunk_rows, c % col_chunks
            piece = chunk_ref[c ^ me].astype(F32) * scale
            cols = slice(k * chunk_cols, (k + 1) * chunk_cols)
            if r < half:
                in_ref[r : r + chunk_rows, cols] = piece
            else:
                out_ref[r - half : r - half + chunk_rows, cols] = piece

    shape = jax.ShapeDtypeStruct((half, 2 * half), F32)
    return call(
        body, (place,), (chunks,), (1,), [whole(chunks.shape)],
        [whole(shape.shape)] * 2, [shape, shape], name="finish_weights",
    )


def stages(peers):
    found, stride = [], 1
    while stride < peers:
        radix = min(4, peers // stride)
        found.append((stride, radix))
        stride *= radix
    return found


def hop(value, peers, offset):
    return lax.ppermute(value, "dom", [(i, i ^ offset) for i in range(peers)])


def sum_over_dom(chunks):
    peers, chunk_rows, chunk_cols = chunks.shape
    plan = stages(peers)
    held = chunks
    for stride, radix in plan:
        parts = held.reshape(-1, radix, chunk_rows, chunk_cols)
        arrived = [hop(parts[:, t], peers, t * stride) for t in range(1, radix)]
        total = parts[:, 0].astype(F32)
        for piece in arrived:
            total = total + piece.astype(F32)
        held = total.astype(BF16)
    held = held.reshape(1, chunk_rows, chunk_cols)
    for stride, radix in reversed(plan):
        arrived = [held] + [hop(held, peers, t * stride) for t in range(1, radix)]
        held = jnp.stack(arrived, axis=1).reshape(-1, chunk_rows, chunk_cols)
    return held


def exchange(sending):
    return lax.all_to_all(sending, "dom", split_axis=0, concat_axis=0, tiled=True)


def swap(value):
    return lax.ppermute(value, "hid", SWAP)


def per_device(
    features,
    history,
    remote_tiles,
    remote_dst,
    serve_block,
    push_flag,
    local_tiles,
    local_src,
    local_dst,
    weight_in,
    weight_out,
    cotangent,
):
    tile = remote_tiles.shape[-1]
    rows, half = features.shape
    count = rows // tile
    peers = remote_tiles.shape[1]
    tiles_remote, tiles_local = remote_tiles[0], local_tiles[0]
    targets_remote, served_ids, flags = remote_dst[0], serve_block[0], push_flag[0]
    sources_local, targets_local = local_src[0], local_dst[0]
    side = lax.axis_index("hid")
    place = jnp.stack([lax.axis_index("dom"), side]).astype(jnp.int32)

    def blocks(values):
        return values.reshape(count, tile, half)

    def own_first(weight):
        joined = jnp.concatenate([weight, swap(weight)], axis=0)
        turned = jnp.concatenate([joined[:, half:], joined[:, :half]], axis=1)
        return jnp.where(side == 0, joined, turned)

    feat_blocks, grad_blocks = blocks(features), blocks(cotangent)
    received = exchange(pick_blocks(served_ids, feat_blocks))
    back = remote_back(targets_remote, tiles_remote, grad_blocks)
    base_forward, base_back = local_both(sources_local, targets_local, tiles_local, feat_blocks, grad_blocks)
    w_in, w_out = own_first(weight_in), own_first(weight_out)
    hist_out = dot(history, w_out[:half, :half]) + dot(swap(history), w_out[half:, :half])
    hist_out = blocks(hist_out.astype(BF16))

    returned = exchange(back)
    z_first = remote_forward(targets_remote, tiles_remote, received, base_forward).reshape(rows, half)
    pre, hidden, hidden_out, sending = middle(
        served_ids, flags, z_first, swap(z_first), w_in, w_out, hist_out
    )
    supplied = exchange(sending)

    base_out = local_forward(sources_local, targets_local, tiles_local, hidden_out)
    sums = gather_grads(served_ids, flags, returned, base_back).reshape(2, rows, half)
    grad_hidden, chunks = backward(
        place, sums, swap(sums), hidden, history, z_first, pre, w_out, peers
    )
    scale = float(rows * peers) ** (-0.5)
    grad_in, grad_out = finish_weights(place, sum_over_dom(chunks), half, scale)
    out = remote_forward(targets_remote, tiles_remote, supplied, base_out).reshape(rows, half)
    return (out, grad_hidden, grad_in, grad_out)


def solution(mesh):
    return jax.shard_map(
        per_device,
        mesh=mesh,
        in_specs=(
            P("dom", "hid"),
            P("dom", "hid"),
            P("dom", None, None, None),
            P("dom", None),
            P("dom", None),
            P("dom", None),
            P("dom", None, None, None),
            P("dom", None),
            P("dom", None),
            P("hid", None),
            P("hid", None),
            P("dom", "hid"),
        ),
        out_specs=(P("dom", "hid"), P("dom", "hid"), P("hid", None), P("hid", None)),
        check_vma=False,
    )
```

```python
import math

import jax
import jax.numpy as jnp
from jax import lax
from jax.experimental import pallas as pl
from jax.experimental.pallas import tpu as pltpu
from jax.sharding import PartitionSpec as P

BF16 = jnp.bfloat16
F32 = jnp.float32
VMEM_SPARE = 6 * 1024 * 1024
VMEM_MOST = 60 * 1024 * 1024
SWAP = ((0, 1), (1, 0))


def dot(a, b):
    return jnp.dot(a, b, preferred_element_type=F32)


def dot_t(a, b):
    return lax.dot_general(a, b, (((0,), (0,)), ((), ())), preferred_element_type=F32)


def dot_nt(a, b):
    return lax.dot_general(a, b, (((1,), (1,)), ((), ())), preferred_element_type=F32)


def call(body, scalars, arrays, grid, in_specs, out_specs, out_shape, scratch=(), flops=0, name=None, vmem=None):
    if vmem is None:
        vmem = VMEM_SPARE + 2 * sum(math.prod(spec.block_shape) * a.dtype.itemsize for spec, a in zip(in_specs, arrays))
        vmem += 2 * sum(
            math.prod(spec.block_shape) * s.dtype.itemsize
            for spec, s in zip(jax.tree.leaves(out_specs), jax.tree.leaves(out_shape))
        )
        vmem += sum(math.prod(s.shape) * jnp.dtype(s.dtype).itemsize for s in scratch)
    moved = sum(a.size * a.dtype.itemsize for a in arrays)
    moved += sum(s.size * s.dtype.itemsize for s in jax.tree.leaves(out_shape))
    return pl.pallas_call(
        body,
        grid_spec=pltpu.PrefetchScalarGridSpec(
            num_scalar_prefetch=len(scalars),
            grid=grid,
            in_specs=in_specs,
            out_specs=out_specs,
            scratch_shapes=list(scratch),
        ),
        out_shape=out_shape,
        compiler_params=pltpu.CompilerParams(vmem_limit_bytes=vmem),
        cost_estimate=pl.CostEstimate(flops=int(flops), bytes_accessed=int(moved), transcendentals=0),
        name=name,
    )(*scalars, *arrays)


def whole(shape):
    return pl.BlockSpec(shape, lambda i, *_: (0,) * len(shape))


def lead(shape):
    return pl.BlockSpec(shape, lambda i, *_: (i,) + (0,) * (len(shape) - 1))


def group_of(peers):
    return 8 if peers % 8 == 0 else 1


def prepare(ids, targets, tiles, nodes, grads):
    peers, tile, _ = tiles.shape
    width = nodes.shape[2]
    group = group_of(peers)

    def body(ids_ref, dst_ref, tiles_ref, nodes_ref, grads_ref, out_ref):
        step = pl.program_id(0)
        for j in range(group):
            out_ref[j, :tile] = nodes_ref[ids_ref[step * group + j]]
            out_ref[j, tile:] = dot_t(tiles_ref[j], grads_ref[dst_ref[step * group + j]]).astype(BF16)

    return call(
        body, (ids, targets), (tiles, nodes, grads), (peers // group,),
        [lead((group, tile, tile)), whole(nodes.shape), whole(grads.shape)], lead((group, 2 * tile, width)),
        jax.ShapeDtypeStruct((peers, 2 * tile, width), BF16),
        flops=2 * peers * tile * tile * width, name="prepare", vmem=VMEM_MOST,
    )


def local_both(sources, targets, tiles, nodes, grads):
    many, tile, _ = tiles.shape
    group = group_of(many)

    def body(src_ref, dst_ref, tiles_ref, nodes_ref, grads_ref, fwd_ref, bwd_ref):
        step = pl.program_id(0)

        @pl.when(step == 0)
        def _():
            fwd_ref[...] = jnp.zeros_like(fwd_ref)
            bwd_ref[...] = jnp.zeros_like(bwd_ref)

        for j in range(group):
            src = src_ref[step * group + j]
            dst = dst_ref[step * group + j]
            fwd_ref[dst] += dot(tiles_ref[j], nodes_ref[src])
            bwd_ref[src] += dot_t(tiles_ref[j], grads_ref[dst])

    shape = jax.ShapeDtypeStruct(nodes.shape, F32)
    return call(
        body, (sources, targets), (tiles, nodes, grads), (many // group,),
        [lead((group, tile, tile)), whole(nodes.shape), whole(grads.shape)],
        [whole(nodes.shape)] * 2, [shape, shape],
        flops=4 * many * tile * tile * nodes.shape[2], name="local_both",
    )


def local_forward(sources, targets, tiles, nodes):
    many, tile, _ = tiles.shape
    group = group_of(many)

    def body(src_ref, dst_ref, tiles_ref, nodes_ref, fwd_ref):
        step = pl.program_id(0)

        @pl.when(step == 0)
        def _():
            fwd_ref[...] = jnp.zeros_like(fwd_ref)

        for j in range(group):
            src = src_ref[step * group + j]
            dst = dst_ref[step * group + j]
            fwd_ref[dst] += dot(tiles_ref[j], nodes_ref[src])

    return call(
        body, (sources, targets), (tiles, nodes), (many // group,),
        [lead((group, tile, tile)), whole(nodes.shape)],
        whole(nodes.shape), jax.ShapeDtypeStruct(nodes.shape, F32),
        flops=2 * many * tile * tile * nodes.shape[2], name="local_forward",
    )


def remote_forward(targets, tiles, received, base):
    peers, tile, _ = tiles.shape
    width = received.shape[2]
    group = group_of(peers)
    steps = peers // group

    def body(dst_ref, tiles_ref, recv_ref, base_ref, out_ref, acc_ref):
        step = pl.program_id(0)

        @pl.when(step == 0)
        def _():
            acc_ref[...] = base_ref[...]

        for j in range(group):
            acc_ref[dst_ref[step * group + j]] += dot(tiles_ref[j], recv_ref[j])

        @pl.when(step == steps - 1)
        def _():
            out_ref[...] = acc_ref[...].astype(BF16)

    return call(
        body, (targets,), (tiles, received, base), (steps,),
        [lead((group, tile, tile)), lead((group, tile, width)), whole(base.shape)],
        whole(base.shape), jax.ShapeDtypeStruct(base.shape, BF16),
        [pltpu.VMEM(base.shape, F32)],
        flops=2 * peers * tile * tile * width, name="remote_forward",
    )


def silu_parts(z_mine, z_other, w_in):
    half = z_mine.shape[1]
    pre = dot(z_mine, w_in[:half]) + dot(z_other, w_in[half:])
    return pre, 1.0 / (1.0 + jnp.exp(-pre))


def middle(ids, flags, z_mine, z_other, w_in, w_out, hist_out):
    rows, half = z_mine.shape
    peers = ids.shape[0]
    count, tile, _ = hist_out.shape
    per = 2 if count % 2 == 0 else 1
    steps = count // per
    span = per * tile

    def body(ids_ref, flag_ref, zm_ref, zo_ref, wi_ref, wo_ref, hw_ref, prod_ref, send_ref):
        step = pl.program_id(0)
        pre, s = silu_parts(zm_ref[...], zo_ref[...], wi_ref[...])
        prod = dot((pre * s).astype(BF16), wo_ref[:, :half]).astype(BF16)
        for j in range(per):
            prod_ref[step * per + j] = prod[j * tile : (j + 1) * tile]

        @pl.when(step == steps - 1)
        def _():
            for p in range(peers):
                fresh = flag_ref[p] == 1
                block = ids_ref[p]

                @pl.when(fresh)
                def _():
                    send_ref[p] = prod_ref[block]

                @pl.when(jnp.logical_not(fresh))
                def _():
                    send_ref[p] = hw_ref[block]

    return call(
        body, (ids, flags), (z_mine, z_other, w_in, w_out, hist_out), (steps,),
        [lead((span, half)), lead((span, half)), whole(w_in.shape), whole(w_out.shape), whole(hist_out.shape)],
        [whole(hist_out.shape), whole((peers, tile, half))],
        [
            jax.ShapeDtypeStruct(hist_out.shape, BF16),
            jax.ShapeDtypeStruct((peers, tile, half), BF16),
        ],
        flops=12 * rows * half * half, name="middle",
    )


def gather_grads(ids, flags, returned, base):
    peers = returned.shape[0]
    count, tile, width = base.shape
    group = group_of(peers)
    steps = peers // group

    def body(ids_ref, flag_ref, ret_ref, base_ref, out_ref, acc_ref):
        step = pl.program_id(0)

        @pl.when(step == 0)
        def _():
            acc_ref[0] = base_ref[...]
            acc_ref[1] = jnp.zeros_like(base_ref)

        for j in range(group):
            p = step * group + j
            side = jnp.where(flag_ref[p] == 1, 0, 1)
            acc_ref[side, ids_ref[p]] += ret_ref[j].astype(F32)

        @pl.when(step == steps - 1)
        def _():
            out_ref[...] = acc_ref[...].astype(BF16)

    both = (2,) + base.shape
    return call(
        body, (ids, flags), (returned, base), (steps,),
        [pl.BlockSpec((group, tile, width), lambda i, *_: (i, 1, 0)), whole(base.shape)],
        whole(both), jax.ShapeDtypeStruct(both, BF16),
        [pltpu.VMEM(both, F32)], name="gather_grads",
    )


def chunking(peers, total, width):
    row_chunks = min(peers, total // 16)
    col_chunks = peers // row_chunks
    return row_chunks, col_chunks, total // row_chunks, width // col_chunks


def backward(place, sums_mine, sums_other, history, z_mine, z_other, w_in, w_out, peers):
    _, rows, half = sums_mine.shape
    step_rows = rows // 4
    row_chunks, col_chunks, chunk_rows, chunk_cols = chunking(peers, 2 * half, 2 * half)

    def body(place_ref, sm_ref, so_ref, hist_ref, zm_ref, zo_ref, wi_ref, wo_ref, gh_ref, chunk_ref, acc_ref):
        step = pl.program_id(0)
        me, side = place_ref[0], place_ref[1]

        @pl.when(step == 0)
        def _():
            acc_ref[...] = jnp.zeros_like(acc_ref)

        z = zm_ref[...]
        pre, s = silu_parts(z, zo_ref[...], wi_ref[...])
        dh = dot_nt(sm_ref[0], wo_ref[:, :half]) + dot_nt(so_ref[0], wo_ref[:, half:])
        gh_ref[...] = dh[:, :half].astype(BF16)
        dpre = (dh * s * (1.0 + pre * (1.0 - s))).astype(BF16)
        hid = (pre[:, :half] * s[:, :half]).astype(BF16)
        hist = hist_ref[...]
        own = pl.ds(pl.multiple_of(side * half, half), half)
        far = pl.ds(pl.multiple_of((1 - side) * half, half), half)
        acc_ref[:half, own] += dot_t(z, dpre[:, :half])
        acc_ref[:half, far] += dot_t(z, dpre[:, half:])
        acc_ref[half:, own] += dot_t(hid, sm_ref[0]) + dot_t(hist, sm_ref[1])
        acc_ref[half:, far] += dot_t(hid, so_ref[0]) + dot_t(hist, so_ref[1])

        @pl.when(step == 3)
        def _():
            for c in range(peers):
                r, k = c // col_chunks, c % col_chunks
                piece = acc_ref[r * chunk_rows : (r + 1) * chunk_rows, k * chunk_cols : (k + 1) * chunk_cols]
                chunk_ref[c ^ me] = piece.astype(BF16)

    sums_spec = pl.BlockSpec((2, step_rows, half), lambda i, *_: (0, i, 0))
    some = lead((step_rows, half))
    return call(
        body, (place,), (sums_mine, sums_other, history, z_mine, z_other, w_in, w_out), (4,),
        [sums_spec, sums_spec, some, some, some, whole(w_in.shape), whole(w_out.shape)],
        [some, whole((peers, chunk_rows, chunk_cols))],
        [
            jax.ShapeDtypeStruct((rows, half), BF16),
            jax.ShapeDtypeStruct((peers, chunk_rows, chunk_cols), BF16),
        ],
        [pltpu.VMEM((2 * half, 2 * half), F32)],
        flops=28 * rows * half * half, name="backward",
    )


def finish_weights(place, chunks, half, scale):
    peers, chunk_rows, chunk_cols = chunks.shape
    _, col_chunks, _, _ = chunking(peers, 2 * half, 2 * half)

    def body(place_ref, chunk_ref, in_ref, out_ref):
        me = place_ref[0]
        for c in range(peers):
            r, k = (c // col_chunks) * chunk_rows, c % col_chunks
            piece = chunk_ref[c ^ me].astype(F32) * scale
            cols = slice(k * chunk_cols, (k + 1) * chunk_cols)
            if r < half:
                in_ref[r : r + chunk_rows, cols] = piece
            else:
                out_ref[r - half : r - half + chunk_rows, cols] = piece

    shape = jax.ShapeDtypeStruct((half, 2 * half), F32)
    return call(
        body, (place,), (chunks,), (1,), [whole(chunks.shape)],
        [whole(shape.shape)] * 2, [shape, shape], name="finish_weights",
    )


def stages(peers):
    found, stride = [], 1
    while stride < peers:
        radix = min(4, peers // stride)
        found.append((stride, radix))
        stride *= radix
    return found


def hop(value, peers, offset):
    return lax.ppermute(value, "dom", [(i, i ^ offset) for i in range(peers)])


def scatter_stage(held, peers, stride, radix):
    parts = held.reshape((-1, radix) + held.shape[1:])
    return parts[:, 0], [hop(parts[:, t], peers, t * stride) for t in range(1, radix)]


def add_pieces(kept, arrived):
    total = kept.astype(F32)
    for piece in arrived:
        total = total + piece.astype(F32)
    return total.astype(BF16)


def gather_stage(held, peers, stride, radix):
    arrived = [held] + [hop(held, peers, t * stride) for t in range(1, radix)]
    return jnp.stack(arrived, axis=1).reshape((-1,) + held.shape[1:])


def tie(values):
    return lax.optimization_barrier(values)


def exchange(sending):
    return lax.all_to_all(sending, "dom", split_axis=0, concat_axis=0, tiled=True)


def swap(value):
    return lax.ppermute(value, "hid", SWAP)


def per_device(
    features,
    history,
    remote_tiles,
    remote_dst,
    serve_block,
    push_flag,
    local_tiles,
    local_src,
    local_dst,
    weight_in,
    weight_out,
    cotangent,
):
    tile = remote_tiles.shape[-1]
    rows, half = features.shape
    count = rows // tile
    peers = remote_tiles.shape[1]
    tiles_remote, tiles_local = remote_tiles[0], local_tiles[0]
    targets_remote, served_ids, flags = remote_dst[0], serve_block[0], push_flag[0]
    sources_local, targets_local = local_src[0], local_dst[0]
    side = lax.axis_index("hid")
    place = jnp.stack([lax.axis_index("dom"), side]).astype(jnp.int32)

    def blocks(values):
        return values.reshape(count, tile, half)

    def own_first(weight):
        joined = jnp.concatenate([weight, swap(weight)], axis=0)
        turned = jnp.concatenate([joined[:, half:], joined[:, :half]], axis=1)
        return jnp.where(side == 0, joined, turned)

    feat_blocks, grad_blocks = blocks(features), blocks(cotangent)
    first = prepare(served_ids, targets_remote, tiles_remote, feat_blocks, grad_blocks)
    received = exchange(first)
    base_forward, base_back = local_both(sources_local, targets_local, tiles_local, feat_blocks, grad_blocks)
    w_in, w_out = own_first(weight_in), own_first(weight_out)
    hist_out = dot(history, w_out[:half, :half]) + dot(swap(history), w_out[half:, :half])
    hist_out = blocks(hist_out.astype(BF16))

    received, w_in, w_out, hist_out, base_forward, base_back = tie(
        (received, w_in, w_out, hist_out, base_forward, base_back)
    )
    z_first = remote_forward(targets_remote, tiles_remote, received, base_forward).reshape(rows, half)
    z_first, received = tie((z_first, received))
    z_other = swap(z_first)
    sums = gather_grads(served_ids, flags, received, base_back).reshape(2, rows, half)
    sums_other = swap(sums)
    hidden_out, sending = middle(served_ids, flags, z_first, z_other, w_in, w_out, hist_out)
    sending, sums, z_first, z_other = tie((sending, sums, z_first, z_other))
    supplied = exchange(sending)
    grad_hidden, chunks = backward(
        place, sums, sums_other, history, z_first, z_other, w_in, w_out, peers
    )
    plan = stages(peers)
    kept, arrived = scatter_stage(chunks, peers, *plan[0])
    kept, hidden_out = tie((kept, hidden_out))
    base_out = local_forward(sources_local, targets_local, tiles_local, hidden_out)
    kept, base_out = tie((kept, base_out))
    held = add_pieces(kept, arrived)
    for stage in plan[1:]:
        held = add_pieces(*scatter_stage(held, peers, *stage))
    for stage in reversed(plan[1:]):
        held = gather_stage(held, peers, *stage)
    held, supplied = tie((held, supplied))
    held = gather_stage(held, peers, *plan[0])
    out = remote_forward(targets_remote, tiles_remote, supplied, base_out)
    held, out = tie((held, out))
    scale = float(rows * peers) ** (-0.5)
    grad_in, grad_out = finish_weights(place, held, half, scale)
    out = out.reshape(rows, half)
    return (out, grad_hidden, grad_in, grad_out)


def solution(mesh):
    return jax.shard_map(
        per_device,
        mesh=mesh,
        in_specs=(
            P("dom", "hid"),
            P("dom", "hid"),
            P("dom", None, None, None),
            P("dom", None),
            P("dom", None),
            P("dom", None),
            P("dom", None, None, None),
            P("dom", None),
            P("dom", None),
            P("hid", None),
            P("hid", None),
            P("dom", "hid"),
        ),
        out_specs=(P("dom", "hid"), P("dom", "hid"), P("hid", None), P("hid", None)),
        check_vma=False,
    )
```

```python
import math

import jax
import jax.numpy as jnp
from jax import lax
from jax.experimental import pallas as pl
from jax.experimental.pallas import tpu as pltpu
from jax.sharding import PartitionSpec as P

BF16 = jnp.bfloat16
F32 = jnp.float32
VMEM_SPARE = 6 * 1024 * 1024
VMEM_MOST = 60 * 1024 * 1024
SWAP = ((0, 1), (1, 0))


def dot(a, b):
    return jnp.dot(a, b, preferred_element_type=F32)


def dot_t(a, b):
    return lax.dot_general(a, b, (((0,), (0,)), ((), ())), preferred_element_type=F32)


def dot_nt(a, b):
    return lax.dot_general(a, b, (((1,), (1,)), ((), ())), preferred_element_type=F32)


def call(body, scalars, arrays, grid, in_specs, out_specs, out_shape, scratch=(), flops=0, name=None, vmem=None):
    if vmem is None:
        vmem = VMEM_SPARE + 2 * sum(math.prod(spec.block_shape) * a.dtype.itemsize for spec, a in zip(in_specs, arrays))
        vmem += 2 * sum(
            math.prod(spec.block_shape) * s.dtype.itemsize
            for spec, s in zip(jax.tree.leaves(out_specs), jax.tree.leaves(out_shape))
        )
        vmem += sum(math.prod(s.shape) * jnp.dtype(s.dtype).itemsize for s in scratch)
    moved = sum(a.size * a.dtype.itemsize for a in arrays)
    moved += sum(s.size * s.dtype.itemsize for s in jax.tree.leaves(out_shape))
    return pl.pallas_call(
        body,
        grid_spec=pltpu.PrefetchScalarGridSpec(
            num_scalar_prefetch=len(scalars),
            grid=grid,
            in_specs=in_specs,
            out_specs=out_specs,
            scratch_shapes=list(scratch),
        ),
        out_shape=out_shape,
        compiler_params=pltpu.CompilerParams(vmem_limit_bytes=vmem),
        cost_estimate=pl.CostEstimate(flops=int(flops), bytes_accessed=int(moved), transcendentals=0),
        name=name,
    )(*scalars, *arrays)


def direct(body, scalars, arrays, in_spaces, out_shape, out_spaces, scratch=(), flops=0, name=None, vmem=None):
    inside = [a for a, space in zip(arrays + out_shape, in_spaces + out_spaces) if space is pltpu.VMEM]
    sizes = [math.prod(a.shape) * jnp.dtype(a.dtype).itemsize for a in inside]
    sizes += [math.prod(a.shape) * jnp.dtype(a.dtype).itemsize for a in scratch if getattr(a, "memory_space", None) is pltpu.VMEM]
    moved = sum(math.prod(a.shape) * jnp.dtype(a.dtype).itemsize for a in arrays + out_shape)
    return pl.pallas_call(
        body,
        in_specs=[pl.BlockSpec(memory_space=pltpu.SMEM)] * len(scalars)
        + [pl.BlockSpec(memory_space=space) for space in in_spaces],
        out_specs=[pl.BlockSpec(memory_space=space) for space in out_spaces],
        out_shape=out_shape,
        scratch_shapes=list(scratch),
        compiler_params=pltpu.CompilerParams(vmem_limit_bytes=vmem or sum(sizes) + VMEM_SPARE),
        cost_estimate=pl.CostEstimate(flops=int(flops), bytes_accessed=int(moved), transcendentals=0),
        name=name,
    )(*scalars, *arrays)


def each(count, step):
    if count <= 4:
        for i in range(count):
            step(i)
    else:
        pl.loop(0, count)(step)


def whole(shape):
    return pl.BlockSpec(shape, lambda i, *_: (0,) * len(shape))


def lead(shape):
    return pl.BlockSpec(shape, lambda i, *_: (i,) + (0,) * (len(shape) - 1))


def group_of(peers):
    return 8 if peers % 8 == 0 else 1


def prepare(ids, targets, tiles, nodes, grads):
    peers, tile, _ = tiles.shape
    width = nodes.shape[2]
    group = group_of(peers)

    def body(ids_ref, dst_ref, tiles_hbm, nodes_hbm, grads_hbm, out_hbm, tiles_ref, nodes_ref, grads_ref, back_ref, in_sem, tile_sem, pick_sem, out_sem):
        def tiles_in(g):
            part = pl.ds(g * group, group)
            return pltpu.make_async_copy(tiles_hbm.at[part], tiles_ref.at[part], tile_sem.at[g])

        def pick(p):
            return pltpu.make_async_copy(nodes_ref.at[ids_ref[p]], out_hbm.at[p, pl.ds(0, tile)], pick_sem.at[p])

        def give(p):
            return pltpu.make_async_copy(back_ref.at[p], out_hbm.at[p, pl.ds(tile, tile)], out_sem.at[p])

        def picks(g):
            for j in range(group):
                pick(g * group + j).start()

        nodes_in = pltpu.make_async_copy(nodes_hbm, nodes_ref, in_sem.at[0])
        grads_in = pltpu.make_async_copy(grads_hbm, grads_ref, in_sem.at[1])
        nodes_in.start()
        grads_in.start()
        each(peers // group, lambda g: tiles_in(g).start())
        nodes_in.wait()
        each(peers // group, picks)
        grads_in.wait()

        def work(g):
            tiles_in(g).wait()
            for j in range(group):
                p = g * group + j
                back_ref[p] = dot_t(tiles_ref[p], grads_ref[dst_ref[p]]).astype(BF16)
                give(p).start()

        def finish(g):
            for j in range(group):
                give(g * group + j).wait()
                pick(g * group + j).wait()

        each(peers // group, work)
        each(peers // group, finish)

    return direct(
        body, (ids, targets), [tiles, nodes, grads], [pltpu.HBM] * 3,
        [jax.ShapeDtypeStruct((peers, 2 * tile, width), BF16)], [pltpu.HBM],
        [
            pltpu.VMEM(tiles.shape, BF16), pltpu.VMEM(nodes.shape, BF16), pltpu.VMEM(grads.shape, BF16),
            pltpu.VMEM((peers, tile, width), BF16), pltpu.SemaphoreType.DMA((2,)), pltpu.SemaphoreType.DMA((peers // group,)),
            pltpu.SemaphoreType.DMA((peers,)), pltpu.SemaphoreType.DMA((peers,)),
        ],
        flops=2 * peers * tile * tile * width, name="prepare", vmem=VMEM_MOST,
    )[0]


def local_both(sources, targets, tiles, nodes, grads):
    many, tile, _ = tiles.shape
    group = group_of(many)

    def body(src_ref, dst_ref, tiles_ref, nodes_ref, grads_ref, fwd_ref, bwd_ref):
        step = pl.program_id(0)

        @pl.when(step == 0)
        def _():
            fwd_ref[...] = jnp.zeros_like(fwd_ref)
            bwd_ref[...] = jnp.zeros_like(bwd_ref)

        for j in range(group):
            src = src_ref[step * group + j]
            dst = dst_ref[step * group + j]
            fwd_ref[dst] += dot(tiles_ref[j], nodes_ref[src])
            bwd_ref[src] += dot_t(tiles_ref[j], grads_ref[dst])

    shape = jax.ShapeDtypeStruct(nodes.shape, F32)
    return call(
        body, (sources, targets), (tiles, nodes, grads), (many // group,),
        [lead((group, tile, tile)), whole(nodes.shape), whole(grads.shape)],
        [whole(nodes.shape)] * 2, [shape, shape],
        flops=4 * many * tile * tile * nodes.shape[2], name="local_both",
    )


def local_forward(sources, targets, tiles, nodes):
    many, tile, _ = tiles.shape
    group = group_of(many)

    def body(src_ref, dst_ref, tiles_ref, nodes_ref, fwd_ref):
        step = pl.program_id(0)

        @pl.when(step == 0)
        def _():
            fwd_ref[...] = jnp.zeros_like(fwd_ref)

        for j in range(group):
            src = src_ref[step * group + j]
            dst = dst_ref[step * group + j]
            fwd_ref[dst] += dot(tiles_ref[j], nodes_ref[src])

    return call(
        body, (sources, targets), (tiles, nodes), (many // group,),
        [lead((group, tile, tile)), whole(nodes.shape)],
        whole(nodes.shape), jax.ShapeDtypeStruct(nodes.shape, F32),
        flops=2 * many * tile * tile * nodes.shape[2], name="local_forward",
    )


def streamed(received, offset, tile, buffer, sems, group):
    def copy(g):
        part = pl.ds(g * group, group)
        return pltpu.make_async_copy(received.at[part, pl.ds(offset, tile)], buffer.at[part], sems.at[g])

    return copy


def remote_forward(targets, tiles, received, base):
    peers, tile, _ = tiles.shape
    width = received.shape[2]
    group = 4 if peers % 4 == 0 else 1

    def body(dst_ref, tiles_ref, recv_hbm, base_ref, out_ref, recv_ref, acc_ref, sems):
        copy = streamed(recv_hbm, 0, tile, recv_ref, sems, group)
        each(peers // group, lambda g: copy(g).start())
        acc_ref[...] = base_ref[...]

        def work(g):
            copy(g).wait()
            for j in range(group):
                p = g * group + j
                acc_ref[dst_ref[p]] += dot(tiles_ref[p], recv_ref[p])

        each(peers // group, work)
        out_ref[...] = acc_ref[...].astype(BF16)

    return direct(
        body, (targets,), [tiles, received, base], [pltpu.VMEM, pltpu.HBM, pltpu.VMEM],
        [jax.ShapeDtypeStruct(base.shape, BF16)], [pltpu.VMEM],
        [
            pltpu.VMEM((peers, tile, width), BF16), pltpu.VMEM(base.shape, F32),
            pltpu.SemaphoreType.DMA((peers // group,)),
        ],
        flops=2 * peers * tile * tile * width, name="remote_forward",
    )[0]


def layer_one(z_mine, z_other, w_in):
    half = z_mine.shape[1]
    pre = dot(z_mine, w_in[:half]) + dot(z_other, w_in[half:])
    return pre, 0.5 * jnp.tanh(0.5 * pre) + 0.5


def middle(ids, flags, z_mine, z_other, w_in, w_out, hist_out):
    rows, half = z_mine.shape
    peers = ids.shape[0]
    count, tile, _ = hist_out.shape
    group = group_of(peers)

    def body(ids_ref, flag_ref, zm_ref, zo_ref, wi_ref, wo_ref, hw_ref, prod_ref, send_hbm, sems):
        def supply(source, p):
            return pltpu.make_async_copy(source.at[ids_ref[p]], send_hbm.at[p], sems.at[p])

        def stored(g):
            for j in range(group):
                p = g * group + j
                pl.when(flag_ref[p] != 1)(lambda: supply(hw_ref, p).start())

        def fresh(g):
            for j in range(group):
                p = g * group + j
                pl.when(flag_ref[p] == 1)(lambda: supply(prod_ref, p).start())

        def finish(g):
            for j in range(group):
                supply(hw_ref, g * group + j).wait()

        each(peers // group, stored)
        per = 2 if count % 2 == 0 else 1
        for r in range(count // per):
            part = slice(r * per * tile, (r + 1) * per * tile)
            pre, s = layer_one(zm_ref[part], zo_ref[part], wi_ref)
            prod = dot((pre * s).astype(BF16), wo_ref[:, :half]).astype(BF16)
            prod_ref[r * per : (r + 1) * per] = prod.reshape(per, tile, half)
        each(peers // group, fresh)
        each(peers // group, finish)

    return direct(
        body, (ids, flags), [z_mine, z_other, w_in, w_out, hist_out], [pltpu.VMEM] * 5,
        [
            jax.ShapeDtypeStruct(hist_out.shape, BF16),
            jax.ShapeDtypeStruct((peers, tile, half), BF16),
        ],
        [pltpu.VMEM, pltpu.HBM],
        [pltpu.SemaphoreType.DMA((peers,))],
        flops=120 * rows * half * half, name="middle",
    )


def gather_grads(ids, flags, returned, base):
    peers = returned.shape[0]
    count, tile, width = base.shape
    group = 4 if peers % 4 == 0 else 1
    both = (2,) + base.shape

    def body(ids_ref, flag_ref, ret_hbm, base_ref, out_ref, ret_ref, acc_ref, sems):
        copy = streamed(ret_hbm, tile, tile, ret_ref, sems, group)
        each(peers // group, lambda g: copy(g).start())
        acc_ref[0] = base_ref[...]
        acc_ref[1] = jnp.zeros_like(base_ref)

        def work(g):
            copy(g).wait()
            for j in range(group):
                p = g * group + j
                side = jnp.where(flag_ref[p] == 1, 0, 1)
                acc_ref[side, ids_ref[p]] += ret_ref[p].astype(F32)

        each(peers // group, work)
        out_ref[...] = acc_ref[...].astype(BF16)

    return direct(
        body, (ids, flags), [returned, base], [pltpu.HBM, pltpu.VMEM],
        [jax.ShapeDtypeStruct(both, BF16)], [pltpu.VMEM],
        [
            pltpu.VMEM((peers, tile, width), BF16), pltpu.VMEM(both, F32),
            pltpu.SemaphoreType.DMA((peers // group,)),
        ],
        flops=32 * peers * tile * tile * width, name="gather_grads",
    )[0]


def chunking(peers, total, width):
    row_chunks = min(peers, total // 16)
    col_chunks = peers // row_chunks
    return row_chunks, col_chunks, total // row_chunks, width // col_chunks


def backward(place, sums_mine, sums_other, history, z_mine, z_other, w_in, w_out, peers):
    _, rows, half = sums_mine.shape
    row_chunks, col_chunks, chunk_rows, chunk_cols = chunking(peers, 2 * half, 2 * half)
    parts = 4
    span = rows // parts

    def body(place_ref, sm_hbm, so_hbm, hist_ref, zm_ref, zo_ref, wi_ref, wo_ref, gh_hbm, chunk_ref, sm_ref, so_ref, gh_ref, acc_ref, sm_sem, so_sem, gh_sem):
        me, side = place_ref[0], place_ref[1]
        own = pl.ds(pl.multiple_of(side * half, half), half)
        far = pl.ds(pl.multiple_of((1 - side) * half, half), half)

        def sums_in(r):
            part = pl.ds(r * span, span)
            return (
                pltpu.make_async_copy(sm_hbm.at[:, part], sm_ref.at[:, part], sm_sem.at[r]),
                pltpu.make_async_copy(so_hbm.at[:, part], so_ref.at[:, part], so_sem.at[r]),
            )

        def gh_out(r):
            part = pl.ds(r * span, span)
            return pltpu.make_async_copy(gh_ref.at[part], gh_hbm.at[part], gh_sem.at[r])

        for r in range(parts):
            for copy in sums_in(r):
                copy.start()
        for r in range(parts):
            part = slice(r * span, (r + 1) * span)

            def add(rows_, cols, value):
                if r == 0:
                    acc_ref[rows_, cols] = value
                else:
                    acc_ref[rows_, cols] += value

            z, hist = zm_ref[part], hist_ref[part]
            pre, s = layer_one(z, zo_ref[part], wi_ref)
            hid = (pre[:, :half] * s[:, :half]).astype(BF16)
            for copy in sums_in(r):
                copy.wait()
            dh = dot_nt(sm_ref[0, part], wo_ref[:, :half]) + dot_nt(so_ref[0, part], wo_ref[:, half:])
            gh_ref[part] = dh[:, :half].astype(BF16)
            gh_out(r).start()
            dpre = (dh * s * (1.0 + pre * (1.0 - s))).astype(BF16)
            add(slice(0, half), own, dot_t(z, dpre[:, :half]))
            add(slice(0, half), far, dot_t(z, dpre[:, half:]))
            add(slice(half, 2 * half), own, dot_t(hid, sm_ref[0, part]) + dot_t(hist, sm_ref[1, part]))
            add(slice(half, 2 * half), far, dot_t(hid, so_ref[0, part]) + dot_t(hist, so_ref[1, part]))
        for c in range(peers):
            r, k = c // col_chunks, c % col_chunks
            piece = acc_ref[r * chunk_rows : (r + 1) * chunk_rows, k * chunk_cols : (k + 1) * chunk_cols]
            chunk_ref[c ^ me] = piece.astype(BF16)
        for r in range(parts):
            gh_out(r).wait()

    return direct(
        body, (place,), [sums_mine, sums_other, history, z_mine, z_other, w_in, w_out],
        [pltpu.HBM] * 2 + [pltpu.VMEM] * 5,
        [
            jax.ShapeDtypeStruct((rows, half), BF16),
            jax.ShapeDtypeStruct((peers, chunk_rows, chunk_cols), BF16),
        ],
        [pltpu.HBM, pltpu.VMEM],
        [
            pltpu.VMEM(sums_mine.shape, BF16), pltpu.VMEM(sums_mine.shape, BF16),
            pltpu.VMEM((rows, half), BF16), pltpu.VMEM((2 * half, 2 * half), F32),
            pltpu.SemaphoreType.DMA((parts,)), pltpu.SemaphoreType.DMA((parts,)), pltpu.SemaphoreType.DMA((parts,)),
        ],
        flops=28 * rows * half * half, name="backward",
    )


def finish_weights(place, chunks, half, scale):
    peers, chunk_rows, chunk_cols = chunks.shape
    _, col_chunks, _, _ = chunking(peers, 2 * half, 2 * half)

    def body(place_ref, chunk_ref, in_ref, out_ref):
        me = place_ref[0]
        for c in range(peers):
            r, k = (c // col_chunks) * chunk_rows, c % col_chunks
            piece = chunk_ref[c ^ me].astype(F32) * scale
            cols = slice(k * chunk_cols, (k + 1) * chunk_cols)
            if r < half:
                in_ref[r : r + chunk_rows, cols] = piece
            else:
                out_ref[r - half : r - half + chunk_rows, cols] = piece

    shape = jax.ShapeDtypeStruct((half, 2 * half), F32)
    return call(
        body, (place,), (chunks,), (1,), [whole(chunks.shape)],
        [whole(shape.shape)] * 2, [shape, shape], name="finish_weights",
    )


def digit(peers):
    return min(4, peers)


def hop(value, peers, offset):
    return lax.ppermute(value, "dom", [(i, i ^ offset) for i in range(peers)])


def scatter_digit(chunks, peers):
    radix = digit(peers)
    parts = chunks.reshape((-1, radix) + chunks.shape[1:])
    return parts[:, 0], [hop(parts[:, t], peers, t) for t in range(1, radix)]


def add_pieces(kept, arrived):
    total = kept.astype(F32)
    for piece in arrived:
        total = total + piece.astype(F32)
    return total.astype(BF16)


def gather_digit(held, peers):
    arrived = [held] + [hop(held, peers, t) for t in range(1, digit(peers))]
    return jnp.stack(arrived, axis=1).reshape((-1,) + held.shape[1:])


def tie(values):
    return lax.optimization_barrier(values)


def exchange(sending):
    return lax.all_to_all(sending, "dom", split_axis=0, concat_axis=0, tiled=True)


def swap(value):
    return lax.ppermute(value, "hid", SWAP)


def per_device(
    features,
    history,
    remote_tiles,
    remote_dst,
    serve_block,
    push_flag,
    local_tiles,
    local_src,
    local_dst,
    weight_in,
    weight_out,
    cotangent,
):
    tile = remote_tiles.shape[-1]
    rows, half = features.shape
    count = rows // tile
    peers = remote_tiles.shape[1]
    tiles_remote, tiles_local = remote_tiles[0], local_tiles[0]
    targets_remote, served_ids, flags = remote_dst[0], serve_block[0], push_flag[0]
    sources_local, targets_local = local_src[0], local_dst[0]
    side = lax.axis_index("hid")
    place = jnp.stack([lax.axis_index("dom") % digit(peers), side]).astype(jnp.int32)

    def blocks(values):
        return values.reshape(count, tile, half)

    def own_first(weight):
        joined = jnp.concatenate([weight, swap(weight)], axis=0)
        turned = jnp.concatenate([joined[:, half:], joined[:, :half]], axis=1)
        return jnp.where(side == 0, joined, turned)

    feat_blocks, grad_blocks = blocks(features), blocks(cotangent)
    first = prepare(served_ids, targets_remote, tiles_remote, feat_blocks, grad_blocks)
    received = exchange(first)
    base_forward, base_back = local_both(sources_local, targets_local, tiles_local, feat_blocks, grad_blocks)
    w_in, w_out = own_first(weight_in), own_first(weight_out)
    hist_out = dot(history, w_out[:half, :half]) + dot(swap(history), w_out[half:, :half])
    hist_out = blocks(hist_out.astype(BF16))

    received, w_in, w_out, hist_out, base_forward, base_back = tie(
        (received, w_in, w_out, hist_out, base_forward, base_back)
    )
    z_first = remote_forward(targets_remote, tiles_remote, received, base_forward).reshape(rows, half)
    z_first, received = tie((z_first, received))
    z_other = swap(z_first)
    sums = gather_grads(served_ids, flags, received, base_back).reshape(2, rows, half)
    sums_other = swap(sums)
    hidden_out, sending = middle(served_ids, flags, z_first, z_other, w_in, w_out, hist_out)
    sending, sums, z_first, z_other = tie((sending, sums, z_first, z_other))
    supplied = exchange(sending)
    grad_hidden, chunks = backward(
        place, sums, sums_other, history, z_first, z_other, w_in, w_out, peers
    )
    kept, arrived = scatter_digit(chunks, peers)
    kept, hidden_out = tie((kept, hidden_out))
    base_out = local_forward(sources_local, targets_local, tiles_local, hidden_out)
    kept, base_out = tie((kept, base_out))
    held = add_pieces(kept, arrived)
    offset = digit(peers)
    while offset < peers:
        held = add_pieces(held, [hop(held, peers, offset)])
        offset *= 2
    held, supplied = tie((held, supplied))
    held = gather_digit(held, peers)
    out = remote_forward(targets_remote, tiles_remote, supplied, base_out)
    held, out = tie((held, out))
    scale = float(rows * peers) ** (-0.5)
    grad_in, grad_out = finish_weights(place, held, half, scale)
    out = out.reshape(rows, half)
    return (out, grad_hidden, grad_in, grad_out)


def solution(mesh):
    return jax.shard_map(
        per_device,
        mesh=mesh,
        in_specs=(
            P("dom", "hid"),
            P("dom", "hid"),
            P("dom", None, None, None),
            P("dom", None),
            P("dom", None),
            P("dom", None),
            P("dom", None, None, None),
            P("dom", None),
            P("dom", None),
            P("hid", None),
            P("hid", None),
            P("dom", "hid"),
        ),
        out_specs=(P("dom", "hid"), P("dom", "hid"), P("hid", None), P("hid", None)),
        check_vma=False,
    )
```

```python
import math

import jax
import jax.numpy as jnp
from jax import lax
from jax.experimental import pallas as pl
from jax.experimental.pallas import tpu as pltpu
from jax.sharding import PartitionSpec as P

BF16 = jnp.bfloat16
F32 = jnp.float32
VMEM_SPARE = 6 * 1024 * 1024
VMEM_MOST = 60 * 1024 * 1024
SWAP = ((0, 1), (1, 0))


def dot(a, b):
    return jnp.dot(a, b, preferred_element_type=F32)


def dot_t(a, b):
    return lax.dot_general(a, b, (((0,), (0,)), ((), ())), preferred_element_type=F32)


def dot_nt(a, b):
    return lax.dot_general(a, b, (((1,), (1,)), ((), ())), preferred_element_type=F32)


def call(body, scalars, arrays, grid, in_specs, out_specs, out_shape, scratch=(), flops=0, name=None, vmem=None):
    if vmem is None:
        vmem = VMEM_SPARE + 2 * sum(math.prod(spec.block_shape) * a.dtype.itemsize for spec, a in zip(in_specs, arrays))
        vmem += 2 * sum(
            math.prod(spec.block_shape) * s.dtype.itemsize
            for spec, s in zip(jax.tree.leaves(out_specs), jax.tree.leaves(out_shape))
        )
        vmem += sum(math.prod(s.shape) * jnp.dtype(s.dtype).itemsize for s in scratch)
    moved = sum(a.size * a.dtype.itemsize for a in arrays)
    moved += sum(s.size * s.dtype.itemsize for s in jax.tree.leaves(out_shape))
    return pl.pallas_call(
        body,
        grid_spec=pltpu.PrefetchScalarGridSpec(
            num_scalar_prefetch=len(scalars),
            grid=grid,
            in_specs=in_specs,
            out_specs=out_specs,
            scratch_shapes=list(scratch),
        ),
        out_shape=out_shape,
        compiler_params=pltpu.CompilerParams(vmem_limit_bytes=vmem),
        cost_estimate=pl.CostEstimate(flops=int(flops), bytes_accessed=int(moved), transcendentals=0),
        name=name,
    )(*scalars, *arrays)


def direct(body, scalars, arrays, in_spaces, out_shape, out_spaces, scratch=(), flops=0, name=None, vmem=None):
    inside = [a for a, space in zip(arrays + out_shape, in_spaces + out_spaces) if space is pltpu.VMEM]
    sizes = [math.prod(a.shape) * jnp.dtype(a.dtype).itemsize for a in inside]
    sizes += [math.prod(a.shape) * jnp.dtype(a.dtype).itemsize for a in scratch if getattr(a, "memory_space", None) is pltpu.VMEM]
    moved = sum(math.prod(a.shape) * jnp.dtype(a.dtype).itemsize for a in arrays + out_shape)
    return pl.pallas_call(
        body,
        in_specs=[pl.BlockSpec(memory_space=pltpu.SMEM)] * len(scalars)
        + [pl.BlockSpec(memory_space=space) for space in in_spaces],
        out_specs=[pl.BlockSpec(memory_space=space) for space in out_spaces],
        out_shape=out_shape,
        scratch_shapes=list(scratch),
        compiler_params=pltpu.CompilerParams(vmem_limit_bytes=vmem or sum(sizes) + VMEM_SPARE),
        cost_estimate=pl.CostEstimate(flops=int(flops), bytes_accessed=int(moved), transcendentals=0),
        name=name,
    )(*scalars, *arrays)


def each(count, step):
    if count <= 4:
        for i in range(count):
            step(i)
    else:
        pl.loop(0, count)(step)


def whole(shape):
    return pl.BlockSpec(shape, lambda i, *_: (0,) * len(shape))


def lead(shape):
    return pl.BlockSpec(shape, lambda i, *_: (i,) + (0,) * (len(shape) - 1))


def group_of(peers):
    return 8 if peers % 8 == 0 else 1


def prepare(ids, targets, tiles, nodes, grads):
    peers, tile, _ = tiles.shape
    width = nodes.shape[2]
    group = group_of(peers)

    def body(ids_ref, dst_ref, tiles_hbm, nodes_hbm, grads_hbm, out_hbm, tiles_ref, nodes_ref, grads_ref, back_ref, in_sem, tile_sem, pick_sem, out_sem):
        def tiles_in(g):
            part = pl.ds(g * group, group)
            return pltpu.make_async_copy(tiles_hbm.at[part], tiles_ref.at[part], tile_sem.at[g])

        def pick(p):
            return pltpu.make_async_copy(nodes_ref.at[ids_ref[p]], out_hbm.at[p, pl.ds(0, tile)], pick_sem.at[p])

        def give(p):
            return pltpu.make_async_copy(back_ref.at[p], out_hbm.at[p, pl.ds(tile, tile)], out_sem.at[p])

        def picks(g):
            for j in range(group):
                pick(g * group + j).start()

        nodes_in = pltpu.make_async_copy(nodes_hbm, nodes_ref, in_sem.at[0])
        grads_in = pltpu.make_async_copy(grads_hbm, grads_ref, in_sem.at[1])
        nodes_in.start()
        grads_in.start()
        each(peers // group, lambda g: tiles_in(g).start())
        nodes_in.wait()
        each(peers // group, picks)
        grads_in.wait()

        def work(g):
            tiles_in(g).wait()
            for j in range(group):
                p = g * group + j
                back_ref[p] = dot_t(tiles_ref[p], grads_ref[dst_ref[p]]).astype(BF16)
                give(p).start()

        def finish(g):
            for j in range(group):
                give(g * group + j).wait()
                pick(g * group + j).wait()

        each(peers // group, work)
        each(peers // group, finish)

    return direct(
        body, (ids, targets), [tiles, nodes, grads], [pltpu.HBM] * 3,
        [jax.ShapeDtypeStruct((peers, 2 * tile, width), BF16)], [pltpu.HBM],
        [
            pltpu.VMEM(tiles.shape, BF16), pltpu.VMEM(nodes.shape, BF16), pltpu.VMEM(grads.shape, BF16),
            pltpu.VMEM((peers, tile, width), BF16), pltpu.SemaphoreType.DMA((2,)), pltpu.SemaphoreType.DMA((peers // group,)),
            pltpu.SemaphoreType.DMA((peers,)), pltpu.SemaphoreType.DMA((peers,)),
        ],
        flops=2 * peers * tile * tile * width, name="prepare", vmem=VMEM_MOST,
    )[0]


def local_both(sources, targets, tiles, nodes, grads):
    many, tile, _ = tiles.shape
    group = group_of(many)

    def body(src_ref, dst_ref, tiles_ref, nodes_ref, grads_ref, fwd_ref, bwd_ref):
        step = pl.program_id(0)

        @pl.when(step == 0)
        def _():
            fwd_ref[...] = jnp.zeros_like(fwd_ref)
            bwd_ref[...] = jnp.zeros_like(bwd_ref)

        for j in range(group):
            src = src_ref[step * group + j]
            dst = dst_ref[step * group + j]
            fwd_ref[dst] += dot(tiles_ref[j], nodes_ref[src])
            bwd_ref[src] += dot_t(tiles_ref[j], grads_ref[dst])

    shape = jax.ShapeDtypeStruct(nodes.shape, F32)
    return call(
        body, (sources, targets), (tiles, nodes, grads), (many // group,),
        [lead((group, tile, tile)), whole(nodes.shape), whole(grads.shape)],
        [whole(nodes.shape)] * 2, [shape, shape],
        flops=4 * many * tile * tile * nodes.shape[2], name="local_both",
    )


def local_forward(sources, targets, tiles, nodes):
    many, tile, _ = tiles.shape
    group = group_of(many)

    def body(src_ref, dst_ref, tiles_ref, nodes_ref, fwd_ref):
        step = pl.program_id(0)

        @pl.when(step == 0)
        def _():
            fwd_ref[...] = jnp.zeros_like(fwd_ref)

        for j in range(group):
            src = src_ref[step * group + j]
            dst = dst_ref[step * group + j]
            fwd_ref[dst] += dot(tiles_ref[j], nodes_ref[src])

    return call(
        body, (sources, targets), (tiles, nodes), (many // group,),
        [lead((group, tile, tile)), whole(nodes.shape)],
        whole(nodes.shape), jax.ShapeDtypeStruct(nodes.shape, F32),
        flops=2 * many * tile * tile * nodes.shape[2], name="local_forward",
    )


def streamed(received, offset, tile, buffer, sems, group):
    def copy(g):
        part = pl.ds(g * group, group)
        return pltpu.make_async_copy(received.at[part, pl.ds(offset, tile)], buffer.at[part], sems.at[g])

    return copy


def remote_forward(targets, tiles, received, base, stream):
    peers, tile, _ = tiles.shape
    width = received.shape[2]
    group = 4 if peers % 4 == 0 else 1

    def body(dst_ref, tiles_ref, recv_hbm, base_ref, out_ref, acc_ref, *rest):
        if stream:
            recv_ref, sems = rest
            copy = streamed(recv_hbm, 0, tile, recv_ref, sems, group)
            each(peers // group, lambda g: copy(g).start())
        else:
            recv_ref = recv_hbm
        acc_ref[...] = base_ref[...]

        def work(g):
            if stream:
                copy(g).wait()
            for j in range(group):
                p = g * group + j
                acc_ref[dst_ref[p]] += dot(tiles_ref[p], recv_ref[p, :tile])

        each(peers // group, work)
        out_ref[...] = acc_ref[...].astype(BF16)

    scratch = [pltpu.VMEM(base.shape, F32)]
    if stream:
        scratch += [pltpu.VMEM((peers, tile, width), BF16), pltpu.SemaphoreType.DMA((peers // group,))]
    return direct(
        body, (targets,), [tiles, received, base], [pltpu.VMEM, pltpu.HBM if stream else pltpu.VMEM, pltpu.VMEM],
        [jax.ShapeDtypeStruct(base.shape, BF16)], [pltpu.VMEM], scratch,
        flops=2 * peers * tile * tile * width, name="remote_forward",
    )[0]


def layer_one(z_mine, z_other, w_in):
    half = z_mine.shape[1]
    pre = dot(z_mine, w_in[:half]) + dot(z_other, w_in[half:])
    return pre, 0.5 * jnp.tanh(0.5 * pre) + 0.5


def middle(ids, flags, z_mine, z_other, w_in, w_out, hist_out):
    rows, half = z_mine.shape
    peers = ids.shape[0]
    count, tile, _ = hist_out.shape
    group = group_of(peers)

    def body(ids_ref, flag_ref, zm_ref, zo_ref, wi_ref, wo_ref, hw_ref, prod_ref, send_hbm, sems):
        def supply(source, p):
            return pltpu.make_async_copy(source.at[ids_ref[p]], send_hbm.at[p], sems.at[p])

        def stored(g):
            for j in range(group):
                p = g * group + j
                pl.when(flag_ref[p] != 1)(lambda: supply(hw_ref, p).start())

        def fresh(g):
            for j in range(group):
                p = g * group + j
                pl.when(flag_ref[p] == 1)(lambda: supply(prod_ref, p).start())

        def finish(g):
            for j in range(group):
                supply(hw_ref, g * group + j).wait()

        each(peers // group, stored)
        per = 2 if count % 2 == 0 else 1
        for r in range(count // per):
            part = slice(r * per * tile, (r + 1) * per * tile)
            pre, s = layer_one(zm_ref[part], zo_ref[part], wi_ref)
            prod = dot((pre * s).astype(BF16), wo_ref[:, :half]).astype(BF16)
            prod_ref[r * per : (r + 1) * per] = prod.reshape(per, tile, half)
        each(peers // group, fresh)
        each(peers // group, finish)

    return direct(
        body, (ids, flags), [z_mine, z_other, w_in, w_out, hist_out], [pltpu.VMEM] * 5,
        [
            jax.ShapeDtypeStruct(hist_out.shape, BF16),
            jax.ShapeDtypeStruct((peers, tile, half), BF16),
        ],
        [pltpu.VMEM, pltpu.HBM],
        [pltpu.SemaphoreType.DMA((peers,))],
        flops=120 * rows * half * half, name="middle",
    )


def gather_grads(ids, flags, returned, base):
    peers = returned.shape[0]
    count, tile, width = base.shape
    group = 4 if peers % 4 == 0 else 1
    both = (2,) + base.shape

    def body(ids_ref, flag_ref, ret_ref, base_ref, out_ref, acc_ref):
        acc_ref[0] = base_ref[...]
        acc_ref[1] = jnp.zeros_like(base_ref)

        def work(g):
            for j in range(group):
                p = g * group + j
                side = jnp.where(flag_ref[p] == 1, 0, 1)
                acc_ref[side, ids_ref[p]] += ret_ref[p, tile:].astype(F32)

        each(peers // group, work)
        out_ref[...] = acc_ref[...].astype(BF16)

    return direct(
        body, (ids, flags), [returned, base], [pltpu.VMEM, pltpu.VMEM],
        [jax.ShapeDtypeStruct(both, BF16)], [pltpu.VMEM], [pltpu.VMEM(both, F32)],
        flops=32 * peers * tile * tile * width, name="gather_grads",
    )[0]


def chunking(peers, total, width):
    row_chunks = min(peers, total // 16)
    col_chunks = peers // row_chunks
    return row_chunks, col_chunks, total // row_chunks, width // col_chunks


def backward(place, sums_mine, sums_other, history, z_mine, z_other, w_in, w_out, peers):
    _, rows, half = sums_mine.shape
    row_chunks, col_chunks, chunk_rows, chunk_cols = chunking(peers, 2 * half, 2 * half)
    parts = 4
    span = rows // parts

    def body(place_ref, sm_hbm, so_hbm, hist_ref, zm_ref, zo_ref, wi_ref, wo_ref, gh_hbm, chunk_ref, sm_ref, so_ref, gh_ref, acc_ref, sm_sem, so_sem, gh_sem):
        me, side = place_ref[0], place_ref[1]
        own = pl.ds(pl.multiple_of(side * half, half), half)
        far = pl.ds(pl.multiple_of((1 - side) * half, half), half)

        def sums_in(r):
            part = pl.ds(r * span, span)
            return (
                pltpu.make_async_copy(sm_hbm.at[:, part], sm_ref.at[:, part], sm_sem.at[r]),
                pltpu.make_async_copy(so_hbm.at[:, part], so_ref.at[:, part], so_sem.at[r]),
            )

        def gh_out(r):
            part = pl.ds(r * span, span)
            return pltpu.make_async_copy(gh_ref.at[part], gh_hbm.at[part], gh_sem.at[r])

        for r in range(parts):
            for copy in sums_in(r):
                copy.start()
        for r in range(parts):
            part = slice(r * span, (r + 1) * span)

            def add(rows_, cols, value):
                if r == 0:
                    acc_ref[rows_, cols] = value
                else:
                    acc_ref[rows_, cols] += value

            z, hist = zm_ref[part], hist_ref[part]
            pre, s = layer_one(z, zo_ref[part], wi_ref)
            hid = (pre[:, :half] * s[:, :half]).astype(BF16)
            for copy in sums_in(r):
                copy.wait()
            dh = dot_nt(sm_ref[0, part], wo_ref[:, :half]) + dot_nt(so_ref[0, part], wo_ref[:, half:])
            gh_ref[part] = dh[:, :half].astype(BF16)
            gh_out(r).start()
            dpre = (dh * s * (1.0 + pre * (1.0 - s))).astype(BF16)
            add(slice(0, half), own, dot_t(z, dpre[:, :half]))
            add(slice(0, half), far, dot_t(z, dpre[:, half:]))
            add(slice(half, 2 * half), own, dot_t(hid, sm_ref[0, part]) + dot_t(hist, sm_ref[1, part]))
            add(slice(half, 2 * half), far, dot_t(hid, so_ref[0, part]) + dot_t(hist, so_ref[1, part]))
        for c in range(peers):
            r, k = c // col_chunks, c % col_chunks
            piece = acc_ref[r * chunk_rows : (r + 1) * chunk_rows, k * chunk_cols : (k + 1) * chunk_cols]
            chunk_ref[c ^ me] = piece.astype(BF16)
        for r in range(parts):
            gh_out(r).wait()

    return direct(
        body, (place,), [sums_mine, sums_other, history, z_mine, z_other, w_in, w_out],
        [pltpu.HBM] * 2 + [pltpu.VMEM] * 5,
        [
            jax.ShapeDtypeStruct((rows, half), BF16),
            jax.ShapeDtypeStruct((peers, chunk_rows, chunk_cols), BF16),
        ],
        [pltpu.HBM, pltpu.VMEM],
        [
            pltpu.VMEM(sums_mine.shape, BF16), pltpu.VMEM(sums_mine.shape, BF16),
            pltpu.VMEM((rows, half), BF16), pltpu.VMEM((2 * half, 2 * half), F32),
            pltpu.SemaphoreType.DMA((parts,)), pltpu.SemaphoreType.DMA((parts,)), pltpu.SemaphoreType.DMA((parts,)),
        ],
        flops=28 * rows * half * half, name="backward",
    )


def finish_weights(place, chunks, half, scale):
    peers, chunk_rows, chunk_cols = chunks.shape
    _, col_chunks, _, _ = chunking(peers, 2 * half, 2 * half)

    def body(place_ref, chunk_ref, in_ref, out_ref):
        me = place_ref[0]
        for c in range(peers):
            r, k = (c // col_chunks) * chunk_rows, c % col_chunks
            piece = chunk_ref[c ^ me].astype(F32) * scale
            cols = slice(k * chunk_cols, (k + 1) * chunk_cols)
            if r < half:
                in_ref[r : r + chunk_rows, cols] = piece
            else:
                out_ref[r - half : r - half + chunk_rows, cols] = piece

    shape = jax.ShapeDtypeStruct((half, 2 * half), F32)
    return call(
        body, (place,), (chunks,), (1,), [whole(chunks.shape)],
        [whole(shape.shape)] * 2, [shape, shape], name="finish_weights",
    )


def digit(peers):
    return min(4, peers)


def hop(value, peers, offset):
    return lax.ppermute(value, "dom", [(i, i ^ offset) for i in range(peers)])


def scatter_digit(chunks, peers):
    radix = digit(peers)
    parts = chunks.reshape((-1, radix) + chunks.shape[1:])
    return parts[:, 0], [hop(parts[:, t], peers, t) for t in range(1, radix)]


def add_pieces(kept, arrived):
    total = kept.astype(F32)
    for piece in arrived:
        total = total + piece.astype(F32)
    return total.astype(BF16)


def gather_digit(held, peers):
    arrived = [held] + [hop(held, peers, t) for t in range(1, digit(peers))]
    return jnp.stack(arrived, axis=1).reshape((-1,) + held.shape[1:])


def tie(values):
    return lax.optimization_barrier(values)


def exchange(sending):
    return lax.all_to_all(sending, "dom", split_axis=0, concat_axis=0, tiled=True)


def swap(value):
    return lax.ppermute(value, "hid", SWAP)


def per_device(
    features,
    history,
    remote_tiles,
    remote_dst,
    serve_block,
    push_flag,
    local_tiles,
    local_src,
    local_dst,
    weight_in,
    weight_out,
    cotangent,
):
    tile = remote_tiles.shape[-1]
    rows, half = features.shape
    count = rows // tile
    peers = remote_tiles.shape[1]
    tiles_remote, tiles_local = remote_tiles[0], local_tiles[0]
    targets_remote, served_ids, flags = remote_dst[0], serve_block[0], push_flag[0]
    sources_local, targets_local = local_src[0], local_dst[0]
    side = lax.axis_index("hid")
    place = jnp.stack([lax.axis_index("dom") % digit(peers), side]).astype(jnp.int32)

    def blocks(values):
        return values.reshape(count, tile, half)

    def own_first(weight):
        joined = jnp.concatenate([weight, swap(weight)], axis=0)
        turned = jnp.concatenate([joined[:, half:], joined[:, :half]], axis=1)
        return jnp.where(side == 0, joined, turned)

    feat_blocks, grad_blocks = blocks(features), blocks(cotangent)
    first = prepare(served_ids, targets_remote, tiles_remote, feat_blocks, grad_blocks)
    received = exchange(first)
    base_forward, base_back = local_both(sources_local, targets_local, tiles_local, feat_blocks, grad_blocks)
    w_in, w_out = own_first(weight_in), own_first(weight_out)
    hist_out = dot(history, w_out[:half, :half]) + dot(swap(history), w_out[half:, :half])
    hist_out = blocks(hist_out.astype(BF16))

    received, w_in, w_out, hist_out, base_forward, base_back = tie(
        (received, w_in, w_out, hist_out, base_forward, base_back)
    )
    z_first = remote_forward(targets_remote, tiles_remote, received, base_forward, False).reshape(rows, half)
    z_first, received = tie((z_first, received))
    z_other = swap(z_first)
    sums = gather_grads(served_ids, flags, received, base_back).reshape(2, rows, half)
    sums_other = swap(sums)
    hidden_out, sending = middle(served_ids, flags, z_first, z_other, w_in, w_out, hist_out)
    sending, sums, z_first, z_other = tie((sending, sums, z_first, z_other))
    supplied = exchange(sending)
    grad_hidden, chunks = backward(
        place, sums, sums_other, history, z_first, z_other, w_in, w_out, peers
    )
    kept, arrived = scatter_digit(chunks, peers)
    kept, hidden_out = tie((kept, hidden_out))
    base_out = local_forward(sources_local, targets_local, tiles_local, hidden_out)
    kept, base_out = tie((kept, base_out))
    held = add_pieces(kept, arrived)
    offset = digit(peers)
    while offset < peers:
        held = add_pieces(held, [hop(held, peers, offset)])
        offset *= 2
    held, supplied = tie((held, supplied))
    held = gather_digit(held, peers)
    out = remote_forward(targets_remote, tiles_remote, supplied, base_out, True)
    held, out = tie((held, out))
    scale = float(rows * peers) ** (-0.5)
    grad_in, grad_out = finish_weights(place, held, half, scale)
    out = out.reshape(rows, half)
    return (out, grad_hidden, grad_in, grad_out)


def solution(mesh):
    return jax.shard_map(
        per_device,
        mesh=mesh,
        in_specs=(
            P("dom", "hid"),
            P("dom", "hid"),
            P("dom", None, None, None),
            P("dom", None),
            P("dom", None),
            P("dom", None),
            P("dom", None, None, None),
            P("dom", None),
            P("dom", None),
            P("hid", None),
            P("hid", None),
            P("dom", "hid"),
        ),
        out_specs=(P("dom", "hid"), P("dom", "hid"), P("hid", None), P("hid", None)),
        check_vma=False,
    )
```

```python
import math

import jax
import jax.numpy as jnp
from jax import lax
from jax.experimental import pallas as pl
from jax.experimental.pallas import tpu as pltpu
from jax.sharding import PartitionSpec as P

BF16 = jnp.bfloat16
F32 = jnp.float32
VMEM_SPARE = 6 * 1024 * 1024
VMEM_MOST = 60 * 1024 * 1024
SWAP = ((0, 1), (1, 0))


def dot(a, b):
    return jnp.dot(a, b, preferred_element_type=F32)


def dot_t(a, b):
    return lax.dot_general(a, b, (((0,), (0,)), ((), ())), preferred_element_type=F32)


def dot_nt(a, b):
    return lax.dot_general(a, b, (((1,), (1,)), ((), ())), preferred_element_type=F32)


def call(body, scalars, arrays, grid, in_specs, out_specs, out_shape, scratch=(), flops=0, name=None, vmem=None):
    if vmem is None:
        vmem = VMEM_SPARE + 2 * sum(math.prod(spec.block_shape) * a.dtype.itemsize for spec, a in zip(in_specs, arrays))
        vmem += 2 * sum(
            math.prod(spec.block_shape) * s.dtype.itemsize
            for spec, s in zip(jax.tree.leaves(out_specs), jax.tree.leaves(out_shape))
        )
        vmem += sum(math.prod(s.shape) * jnp.dtype(s.dtype).itemsize for s in scratch)
    moved = sum(a.size * a.dtype.itemsize for a in arrays)
    moved += sum(s.size * s.dtype.itemsize for s in jax.tree.leaves(out_shape))
    return pl.pallas_call(
        body,
        grid_spec=pltpu.PrefetchScalarGridSpec(
            num_scalar_prefetch=len(scalars),
            grid=grid,
            in_specs=in_specs,
            out_specs=out_specs,
            scratch_shapes=list(scratch),
        ),
        out_shape=out_shape,
        compiler_params=pltpu.CompilerParams(vmem_limit_bytes=vmem),
        cost_estimate=pl.CostEstimate(flops=int(flops), bytes_accessed=int(moved), transcendentals=0),
        name=name,
    )(*scalars, *arrays)


def direct(body, scalars, arrays, in_spaces, out_shape, out_spaces, scratch=(), flops=0, name=None, vmem=None):
    inside = [a for a, space in zip(arrays + out_shape, in_spaces + out_spaces) if space is pltpu.VMEM]
    sizes = [math.prod(a.shape) * jnp.dtype(a.dtype).itemsize for a in inside]
    sizes += [math.prod(a.shape) * jnp.dtype(a.dtype).itemsize for a in scratch if getattr(a, "memory_space", None) is pltpu.VMEM]
    moved = sum(math.prod(a.shape) * jnp.dtype(a.dtype).itemsize for a in arrays + out_shape)
    return pl.pallas_call(
        body,
        in_specs=[pl.BlockSpec(memory_space=pltpu.SMEM)] * len(scalars)
        + [pl.BlockSpec(memory_space=space) for space in in_spaces],
        out_specs=[pl.BlockSpec(memory_space=space) for space in out_spaces],
        out_shape=out_shape,
        scratch_shapes=list(scratch),
        compiler_params=pltpu.CompilerParams(vmem_limit_bytes=vmem or sum(sizes) + VMEM_SPARE),
        cost_estimate=pl.CostEstimate(flops=int(flops), bytes_accessed=int(moved), transcendentals=0),
        name=name,
    )(*scalars, *arrays)


def each(count, step):
    if count <= 4:
        for i in range(count):
            step(i)
    else:
        pl.loop(0, count)(step)


def whole(shape):
    return pl.BlockSpec(shape, lambda i, *_: (0,) * len(shape))


def lead(shape):
    return pl.BlockSpec(shape, lambda i, *_: (i,) + (0,) * (len(shape) - 1))


def group_of(peers):
    return 8 if peers % 8 == 0 else 1


def prepare(ids, targets, tiles, nodes, grads):
    peers, tile, _ = tiles.shape
    width = nodes.shape[2]
    group = group_of(peers)

    def body(ids_ref, dst_ref, tiles_hbm, nodes_hbm, grads_hbm, out_hbm, tiles_ref, nodes_ref, grads_ref, back_ref, in_sem, tile_sem, pick_sem, out_sem):
        def tiles_in(g):
            part = pl.ds(g * group, group)
            return pltpu.make_async_copy(tiles_hbm.at[part], tiles_ref.at[part], tile_sem.at[g])

        def pick(p):
            return pltpu.make_async_copy(nodes_ref.at[ids_ref[p]], out_hbm.at[p, pl.ds(0, tile)], pick_sem.at[p])

        def give(p):
            return pltpu.make_async_copy(back_ref.at[p], out_hbm.at[p, pl.ds(tile, tile)], out_sem.at[p])

        def picks(g):
            for j in range(group):
                pick(g * group + j).start()

        nodes_in = pltpu.make_async_copy(nodes_hbm, nodes_ref, in_sem.at[0])
        grads_in = pltpu.make_async_copy(grads_hbm, grads_ref, in_sem.at[1])
        nodes_in.start()
        grads_in.start()
        each(peers // group, lambda g: tiles_in(g).start())
        nodes_in.wait()
        each(peers // group, picks)
        grads_in.wait()

        def work(g):
            tiles_in(g).wait()
            for j in range(group):
                p = g * group + j
                back_ref[p] = dot_t(tiles_ref[p], grads_ref[dst_ref[p]]).astype(BF16)
                give(p).start()

        def finish(g):
            for j in range(group):
                give(g * group + j).wait()
                pick(g * group + j).wait()

        each(peers // group, work)
        each(peers // group, finish)

    return direct(
        body, (ids, targets), [tiles, nodes, grads], [pltpu.HBM] * 3,
        [jax.ShapeDtypeStruct((peers, 2 * tile, width), BF16)], [pltpu.HBM],
        [
            pltpu.VMEM(tiles.shape, BF16), pltpu.VMEM(nodes.shape, BF16), pltpu.VMEM(grads.shape, BF16),
            pltpu.VMEM((peers, tile, width), BF16), pltpu.SemaphoreType.DMA((2,)), pltpu.SemaphoreType.DMA((peers // group,)),
            pltpu.SemaphoreType.DMA((peers,)), pltpu.SemaphoreType.DMA((peers,)),
        ],
        flops=2 * peers * tile * tile * width, name="prepare", vmem=VMEM_MOST,
    )[0]


def local_both(sources, targets, tiles, nodes, grads):
    many, tile, _ = tiles.shape
    group = group_of(many)

    def body(src_ref, dst_ref, tiles_ref, nodes_ref, grads_ref, fwd_ref, bwd_ref):
        step = pl.program_id(0)

        @pl.when(step == 0)
        def _():
            fwd_ref[...] = jnp.zeros_like(fwd_ref)
            bwd_ref[...] = jnp.zeros_like(bwd_ref)

        for j in range(group):
            src = src_ref[step * group + j]
            dst = dst_ref[step * group + j]
            fwd_ref[dst] += dot(tiles_ref[j], nodes_ref[src])
            bwd_ref[src] += dot_t(tiles_ref[j], grads_ref[dst])

    shape = jax.ShapeDtypeStruct(nodes.shape, F32)
    return call(
        body, (sources, targets), (tiles, nodes, grads), (many // group,),
        [lead((group, tile, tile)), whole(nodes.shape), whole(grads.shape)],
        [whole(nodes.shape)] * 2, [shape, shape],
        flops=4 * many * tile * tile * nodes.shape[2], name="local_both",
    )


def streamed(received, offset, tile, buffer, sems, group):
    def copy(g):
        part = pl.ds(g * group, group)
        return pltpu.make_async_copy(received.at[part, pl.ds(offset, tile)], buffer.at[part], sems.at[g])

    return copy


def remote_forward(targets, tiles, received, base, stream):
    peers, tile, _ = tiles.shape
    width = received.shape[2]
    group = 4 if peers % 4 == 0 else 1

    def body(dst_ref, tiles_ref, recv_hbm, base_ref, out_ref, acc_ref, *rest):
        if stream:
            recv_ref, sems = rest
            copy = streamed(recv_hbm, 0, tile, recv_ref, sems, group)
            each(peers // group, lambda g: copy(g).start())
        else:
            recv_ref = recv_hbm
        acc_ref[...] = base_ref[...]

        def work(g):
            if stream:
                copy(g).wait()
            for j in range(group):
                p = g * group + j
                acc_ref[dst_ref[p]] += dot(tiles_ref[p], recv_ref[p, :tile])

        each(peers // group, work)
        out_ref[...] = acc_ref[...].astype(BF16)

    scratch = [pltpu.VMEM(base.shape, F32)]
    if stream:
        scratch += [pltpu.VMEM((peers, tile, width), BF16), pltpu.SemaphoreType.DMA((peers // group,))]
    return direct(
        body, (targets,), [tiles, received, base], [pltpu.VMEM, pltpu.HBM if stream else pltpu.VMEM, pltpu.VMEM],
        [jax.ShapeDtypeStruct(base.shape, BF16)], [pltpu.VMEM], scratch,
        flops=2 * peers * tile * tile * width, name="remote_forward",
    )[0]


def layer_one(z_mine, z_other, w_in):
    half = z_mine.shape[1]
    pre = dot(z_mine, w_in[:half]) + dot(z_other, w_in[half:])
    return pre, 0.5 * jnp.tanh(0.5 * pre) + 0.5


def supplied_product(zm_ref, zo_ref, wi_ref, wo_ref, prod_ref):
    count, tile, half = prod_ref.shape
    per = 2 if count % 2 == 0 else 1
    for r in range(count // per):
        part = slice(r * per * tile, (r + 1) * per * tile)
        pre, s = layer_one(zm_ref[part], zo_ref[part], wi_ref)
        prod = dot((pre * s).astype(BF16), wo_ref[:, :half]).astype(BF16)
        prod_ref[r * per : (r + 1) * per] = prod.reshape(per, tile, half)


def middle(ids, flags, z_mine, z_other, w_in, w_out, hist_out):
    rows, half = z_mine.shape
    peers = ids.shape[0]
    count, tile, _ = hist_out.shape
    group = group_of(peers)

    def body(ids_ref, flag_ref, zm_ref, zo_ref, wi_ref, wo_ref, hw_ref, send_hbm, prod_ref, sems):
        def supply(source, p):
            return pltpu.make_async_copy(source.at[ids_ref[p]], send_hbm.at[p], sems.at[p])

        def stored(g):
            for j in range(group):
                p = g * group + j
                pl.when(flag_ref[p] != 1)(lambda: supply(hw_ref, p).start())

        def fresh(g):
            for j in range(group):
                p = g * group + j
                pl.when(flag_ref[p] == 1)(lambda: supply(prod_ref, p).start())

        def finish(g):
            for j in range(group):
                supply(hw_ref, g * group + j).wait()

        each(peers // group, stored)
        supplied_product(zm_ref, zo_ref, wi_ref, wo_ref, prod_ref)
        each(peers // group, fresh)
        each(peers // group, finish)

    return direct(
        body, (ids, flags), [z_mine, z_other, w_in, w_out, hist_out], [pltpu.VMEM] * 5,
        [jax.ShapeDtypeStruct((peers, tile, half), BF16)], [pltpu.HBM],
        [pltpu.VMEM(hist_out.shape, BF16), pltpu.SemaphoreType.DMA((peers,))],
        flops=120 * rows * half * half, name="middle", vmem=61 * 1024 * 1024,
    )[0]


def local_out(sources, targets, tiles, sums_mine, sums_other, w_in, w_out):
    many, tile, _ = tiles.shape
    _, rows, half = sums_mine.shape
    shape = (rows // tile, tile, half)

    def body(src_ref, dst_ref, tiles_ref, sm_hbm, so_hbm, wi_ref, wo_ref, out_ref, zm_ref, zo_ref, prod_ref, sems):
        copies = [
            pltpu.make_async_copy(sm_hbm.at[2], zm_ref, sems.at[0]),
            pltpu.make_async_copy(so_hbm.at[2], zo_ref, sems.at[1]),
        ]
        for copy in copies:
            copy.start()
        for copy in copies:
            copy.wait()
        supplied_product(zm_ref, zo_ref, wi_ref, wo_ref, prod_ref)
        out_ref[...] = jnp.zeros_like(out_ref)
        for k in range(many):
            out_ref[dst_ref[k]] += dot(tiles_ref[k], prod_ref[src_ref[k]])

    return direct(
        body, (sources, targets), [tiles, sums_mine, sums_other, w_in, w_out],
        [pltpu.VMEM] + [pltpu.HBM] * 2 + [pltpu.VMEM] * 2,
        [jax.ShapeDtypeStruct(shape, F32)], [pltpu.VMEM],
        [
            pltpu.VMEM((rows, half), BF16), pltpu.VMEM((rows, half), BF16), pltpu.VMEM(shape, BF16),
            pltpu.SemaphoreType.DMA((2,)),
        ],
        flops=12 * rows * half * half + 2 * many * tile * tile * half, name="local_out",
    )[0]


def gather_grads(ids, flags, returned, base, z_mine):
    peers = returned.shape[0]
    count, tile, width = base.shape
    group = 4 if peers % 4 == 0 else 1
    both = (2,) + base.shape

    def body(ids_ref, flag_ref, ret_ref, base_ref, z_ref, out_ref, acc_ref):
        out_ref[2] = z_ref[...]
        acc_ref[0] = base_ref[...]
        acc_ref[1] = jnp.zeros_like(base_ref)

        def work(g):
            for j in range(group):
                p = g * group + j
                side = jnp.where(flag_ref[p] == 1, 0, 1)
                acc_ref[side, ids_ref[p]] += ret_ref[p, tile:].astype(F32)

        each(peers // group, work)
        out_ref[:2] = acc_ref[...].astype(BF16)

    return direct(
        body, (ids, flags), [returned, base, z_mine], [pltpu.VMEM] * 3,
        [jax.ShapeDtypeStruct((3,) + base.shape, BF16)], [pltpu.VMEM], [pltpu.VMEM(both, F32)],
        flops=32 * peers * tile * tile * width, name="gather_grads",
    )[0]


def chunking(peers, total, width):
    row_chunks = min(peers, total // 16)
    col_chunks = peers // row_chunks
    return row_chunks, col_chunks, total // row_chunks, width // col_chunks


def backward(place, sums_mine, sums_other, history, w_in, w_out, peers):
    _, rows, half = sums_mine.shape
    row_chunks, col_chunks, chunk_rows, chunk_cols = chunking(peers, 2 * half, 2 * half)
    parts = 4
    span = rows // parts

    def body(place_ref, sm_hbm, so_hbm, hist_ref, wi_ref, wo_ref, gh_hbm, chunk_ref, sm_ref, so_ref, gh_ref, acc_ref, sm_sem, so_sem, gh_sem):
        me, side = place_ref[0], place_ref[1]
        own = pl.ds(pl.multiple_of(side * half, half), half)
        far = pl.ds(pl.multiple_of((1 - side) * half, half), half)

        def sums_in(r):
            part = pl.ds(r * span, span)
            return (
                pltpu.make_async_copy(sm_hbm.at[:, part], sm_ref.at[:, part], sm_sem.at[r]),
                pltpu.make_async_copy(so_hbm.at[:, part], so_ref.at[:, part], so_sem.at[r]),
            )

        def gh_out(r):
            part = pl.ds(r * span, span)
            return pltpu.make_async_copy(gh_ref.at[part], gh_hbm.at[part], gh_sem.at[r])

        for r in range(parts):
            for copy in sums_in(r):
                copy.start()
        for r in range(parts):
            part = slice(r * span, (r + 1) * span)

            def add(rows_, cols, value):
                if r == 0:
                    acc_ref[rows_, cols] = value
                else:
                    acc_ref[rows_, cols] += value

            for copy in sums_in(r):
                copy.wait()
            z, hist = sm_ref[2, part], hist_ref[part]
            pre, s = layer_one(z, so_ref[2, part], wi_ref)
            hid = (pre[:, :half] * s[:, :half]).astype(BF16)
            dh = dot_nt(sm_ref[0, part], wo_ref[:, :half]) + dot_nt(so_ref[0, part], wo_ref[:, half:])
            gh_ref[part] = dh[:, :half].astype(BF16)
            gh_out(r).start()
            dpre = (dh * s * (1.0 + pre * (1.0 - s))).astype(BF16)
            add(slice(0, half), own, dot_t(z, dpre[:, :half]))
            add(slice(0, half), far, dot_t(z, dpre[:, half:]))
            add(slice(half, 2 * half), own, dot_t(hid, sm_ref[0, part]) + dot_t(hist, sm_ref[1, part]))
            add(slice(half, 2 * half), far, dot_t(hid, so_ref[0, part]) + dot_t(hist, so_ref[1, part]))
        for c in range(peers):
            r, k = c // col_chunks, c % col_chunks
            piece = acc_ref[r * chunk_rows : (r + 1) * chunk_rows, k * chunk_cols : (k + 1) * chunk_cols]
            chunk_ref[c ^ me] = piece.astype(BF16)
        for r in range(parts):
            gh_out(r).wait()

    return direct(
        body, (place,), [sums_mine, sums_other, history, w_in, w_out],
        [pltpu.HBM] * 2 + [pltpu.VMEM] * 3,
        [
            jax.ShapeDtypeStruct((rows, half), BF16),
            jax.ShapeDtypeStruct((peers, chunk_rows, chunk_cols), BF16),
        ],
        [pltpu.HBM, pltpu.VMEM],
        [
            pltpu.VMEM((3, rows, half), BF16), pltpu.VMEM((3, rows, half), BF16),
            pltpu.VMEM((rows, half), BF16), pltpu.VMEM((2 * half, 2 * half), F32),
            pltpu.SemaphoreType.DMA((parts,)), pltpu.SemaphoreType.DMA((parts,)), pltpu.SemaphoreType.DMA((parts,)),
        ],
        flops=28 * rows * half * half, name="backward",
    )


def finish_weights(place, chunks, half, scale):
    peers, chunk_rows, chunk_cols = chunks.shape
    _, col_chunks, _, _ = chunking(peers, 2 * half, 2 * half)
    steps = 4
    span = half // steps

    def body(place_ref, chunk_ref, in_hbm, out_hbm, all_ref, sems):
        def leave(k):
            target = in_hbm if k < steps else out_hbm
            return pltpu.make_async_copy(
                all_ref.at[pl.ds(k * span, span)], target.at[pl.ds(k % steps * span, span)], sems.at[k]
            )

        me = place_ref[0]
        sent = 0
        for c in range(peers):
            r, k = (c // col_chunks) * chunk_rows, c % col_chunks
            piece = chunk_ref[c ^ me].astype(F32) * scale
            all_ref[r : r + chunk_rows, k * chunk_cols : (k + 1) * chunk_cols] = piece
            if k == col_chunks - 1 and (r + chunk_rows) % span == 0:
                leave(sent).start()
                sent += 1
        for k in range(2 * steps):
            leave(k).wait()

    shape = jax.ShapeDtypeStruct((half, 2 * half), F32)
    return direct(
        body, (place,), [chunks], [pltpu.VMEM], [shape, shape], [pltpu.HBM] * 2,
        [pltpu.VMEM((2 * half, 2 * half), F32), pltpu.SemaphoreType.DMA((2 * steps,))], name="finish_weights",
    )


def digit(peers):
    return min(4, peers)


def hop(value, peers, offset):
    return lax.ppermute(value, "dom", [(i, i ^ offset) for i in range(peers)])


def scatter_digit(chunks, peers):
    radix = digit(peers)
    parts = chunks.reshape((-1, radix) + chunks.shape[1:])
    return parts[:, 0], [hop(parts[:, t], peers, t) for t in range(1, radix)]


def add_pieces(kept, arrived):
    total = kept.astype(F32)
    for piece in arrived:
        total = total + piece.astype(F32)
    return total.astype(BF16)


def gather_digit(held, peers):
    arrived = [held] + [hop(held, peers, t) for t in range(1, digit(peers))]
    return jnp.stack(arrived, axis=1).reshape((-1,) + held.shape[1:])


def tie(values):
    return lax.optimization_barrier(values)


def exchange(sending):
    return lax.all_to_all(sending, "dom", split_axis=0, concat_axis=0, tiled=True)


def swap(value):
    return lax.ppermute(value, "hid", SWAP)


def per_device(
    features,
    history,
    remote_tiles,
    remote_dst,
    serve_block,
    push_flag,
    local_tiles,
    local_src,
    local_dst,
    weight_in,
    weight_out,
    cotangent,
):
    tile = remote_tiles.shape[-1]
    rows, half = features.shape
    count = rows // tile
    peers = remote_tiles.shape[1]
    tiles_remote, tiles_local = remote_tiles[0], local_tiles[0]
    targets_remote, served_ids, flags = remote_dst[0], serve_block[0], push_flag[0]
    sources_local, targets_local = local_src[0], local_dst[0]
    side = lax.axis_index("hid")
    place = jnp.stack([lax.axis_index("dom") % digit(peers), side]).astype(jnp.int32)

    def blocks(values):
        return values.reshape(count, tile, half)

    def own_first(weight):
        joined = jnp.concatenate([weight, swap(weight)], axis=0)
        turned = jnp.concatenate([joined[:, half:], joined[:, :half]], axis=1)
        return jnp.where(side == 0, joined, turned)

    feat_blocks, grad_blocks = blocks(features), blocks(cotangent)
    first = prepare(served_ids, targets_remote, tiles_remote, feat_blocks, grad_blocks)
    received = exchange(first)
    base_forward, base_back = local_both(sources_local, targets_local, tiles_local, feat_blocks, grad_blocks)
    w_in, w_out = own_first(weight_in), own_first(weight_out)
    hist_out = dot(history, w_out[:half, :half]) + dot(swap(history), w_out[half:, :half])
    hist_out = blocks(hist_out.astype(BF16))

    received, w_in, w_out, hist_out, base_forward, base_back = tie(
        (received, w_in, w_out, hist_out, base_forward, base_back)
    )
    z_first = remote_forward(targets_remote, tiles_remote, received, base_forward, False).reshape(rows, half)
    z_first, received = tie((z_first, received))
    z_other = swap(z_first)
    sums = gather_grads(served_ids, flags, received, base_back, blocks(z_first)).reshape(3, rows, half)
    sums_other = swap(sums)
    sending = middle(served_ids, flags, z_first, z_other, w_in, w_out, hist_out)
    sending, sums = tie((sending, sums))
    supplied = exchange(sending)
    grad_hidden, chunks = backward(
        place, sums, sums_other, history, w_in, w_out, peers
    )
    kept, arrived = scatter_digit(chunks, peers)
    kept, sums = tie((kept, sums))
    base_out = local_out(sources_local, targets_local, tiles_local, sums, sums_other, w_in, w_out)
    kept, base_out = tie((kept, base_out))
    held = add_pieces(kept, arrived)
    offset = digit(peers)
    while offset < peers:
        held = add_pieces(held, [hop(held, peers, offset)])
        offset *= 2
    held, supplied = tie((held, supplied))
    held = gather_digit(held, peers)
    out = remote_forward(targets_remote, tiles_remote, supplied, base_out, True)
    held, out = tie((held, out))
    scale = float(rows * peers) ** (-0.5)
    grad_in, grad_out = finish_weights(place, held, half, scale)
    out = out.reshape(rows, half)
    return (out, grad_hidden, grad_in, grad_out)


def solution(mesh):
    return jax.shard_map(
        per_device,
        mesh=mesh,
        in_specs=(
            P("dom", "hid"),
            P("dom", "hid"),
            P("dom", None, None, None),
            P("dom", None),
            P("dom", None),
            P("dom", None),
            P("dom", None, None, None),
            P("dom", None),
            P("dom", None),
            P("hid", None),
            P("hid", None),
            P("dom", "hid"),
        ),
        out_specs=(P("dom", "hid"), P("dom", "hid"), P("hid", None), P("hid", None)),
        check_vma=False,
    )
```

```python
import math

import jax
import jax.numpy as jnp
from jax import lax
from jax.experimental import pallas as pl
from jax.experimental.pallas import tpu as pltpu
from jax.sharding import PartitionSpec as P

BF16 = jnp.bfloat16
F32 = jnp.float32
VMEM_SPARE = 6 * 1024 * 1024
VMEM_MOST = 60 * 1024 * 1024
SWAP = ((0, 1), (1, 0))


def dot(a, b):
    return jnp.dot(a, b, preferred_element_type=F32)


def dot_t(a, b):
    return lax.dot_general(a, b, (((0,), (0,)), ((), ())), preferred_element_type=F32)


def dot_nt(a, b):
    return lax.dot_general(a, b, (((1,), (1,)), ((), ())), preferred_element_type=F32)


def call(body, scalars, arrays, grid, in_specs, out_specs, out_shape, scratch=(), flops=0, name=None, vmem=None):
    if vmem is None:
        vmem = VMEM_SPARE + 2 * sum(math.prod(spec.block_shape) * a.dtype.itemsize for spec, a in zip(in_specs, arrays))
        vmem += 2 * sum(
            math.prod(spec.block_shape) * s.dtype.itemsize
            for spec, s in zip(jax.tree.leaves(out_specs), jax.tree.leaves(out_shape))
        )
        vmem += sum(math.prod(s.shape) * jnp.dtype(s.dtype).itemsize for s in scratch)
    moved = sum(a.size * a.dtype.itemsize for a in arrays)
    moved += sum(s.size * s.dtype.itemsize for s in jax.tree.leaves(out_shape))
    return pl.pallas_call(
        body,
        grid_spec=pltpu.PrefetchScalarGridSpec(
            num_scalar_prefetch=len(scalars),
            grid=grid,
            in_specs=in_specs,
            out_specs=out_specs,
            scratch_shapes=list(scratch),
        ),
        out_shape=out_shape,
        compiler_params=pltpu.CompilerParams(vmem_limit_bytes=vmem),
        cost_estimate=pl.CostEstimate(flops=int(flops), bytes_accessed=int(moved), transcendentals=0),
        name=name,
    )(*scalars, *arrays)


def direct(body, scalars, arrays, in_spaces, out_shape, out_spaces, scratch=(), flops=0, name=None, vmem=None):
    inside = [a for a, space in zip(arrays + out_shape, in_spaces + out_spaces) if space is pltpu.VMEM]
    sizes = [math.prod(a.shape) * jnp.dtype(a.dtype).itemsize for a in inside]
    sizes += [math.prod(a.shape) * jnp.dtype(a.dtype).itemsize for a in scratch if getattr(a, "memory_space", None) is pltpu.VMEM]
    moved = sum(math.prod(a.shape) * jnp.dtype(a.dtype).itemsize for a in arrays + out_shape)
    return pl.pallas_call(
        body,
        in_specs=[pl.BlockSpec(memory_space=pltpu.SMEM)] * len(scalars)
        + [pl.BlockSpec(memory_space=space) for space in in_spaces],
        out_specs=[pl.BlockSpec(memory_space=space) for space in out_spaces],
        out_shape=out_shape,
        scratch_shapes=list(scratch),
        compiler_params=pltpu.CompilerParams(vmem_limit_bytes=vmem or sum(sizes) + VMEM_SPARE),
        cost_estimate=pl.CostEstimate(flops=int(flops), bytes_accessed=int(moved), transcendentals=0),
        name=name,
    )(*scalars, *arrays)


def each(count, step):
    if count <= 4:
        for i in range(count):
            step(i)
    else:
        pl.loop(0, count)(step)


def whole(shape):
    return pl.BlockSpec(shape, lambda i, *_: (0,) * len(shape))


def lead(shape):
    return pl.BlockSpec(shape, lambda i, *_: (i,) + (0,) * (len(shape) - 1))


def group_of(peers):
    return 8 if peers % 8 == 0 else 1


def prepare(ids, targets, tiles, nodes, grads):
    peers, tile, _ = tiles.shape
    width = nodes.shape[2]
    group = group_of(peers)

    def body(ids_ref, dst_ref, tiles_hbm, nodes_hbm, grads_hbm, out_hbm, tiles_ref, nodes_ref, grads_ref, back_ref, in_sem, tile_sem, pick_sem, out_sem):
        def tiles_in(g):
            part = pl.ds(g * group, group)
            return pltpu.make_async_copy(tiles_hbm.at[part], tiles_ref.at[part], tile_sem.at[g])

        def pick(p):
            return pltpu.make_async_copy(nodes_ref.at[ids_ref[p]], out_hbm.at[p, pl.ds(0, tile)], pick_sem.at[p])

        def give(p):
            return pltpu.make_async_copy(back_ref.at[p], out_hbm.at[p, pl.ds(tile, tile)], out_sem.at[p])

        def picks(g):
            for j in range(group):
                pick(g * group + j).start()

        nodes_in = pltpu.make_async_copy(nodes_hbm, nodes_ref, in_sem.at[0])
        grads_in = pltpu.make_async_copy(grads_hbm, grads_ref, in_sem.at[1])
        nodes_in.start()
        grads_in.start()
        each(peers // group, lambda g: tiles_in(g).start())
        nodes_in.wait()
        each(peers // group, picks)
        grads_in.wait()

        def work(g):
            tiles_in(g).wait()
            for j in range(group):
                p = g * group + j
                back_ref[p] = dot_t(tiles_ref[p], grads_ref[dst_ref[p]]).astype(BF16)
                give(p).start()

        def finish(g):
            for j in range(group):
                give(g * group + j).wait()
                pick(g * group + j).wait()

        each(peers // group, work)
        each(peers // group, finish)

    return direct(
        body, (ids, targets), [tiles, nodes, grads], [pltpu.HBM] * 3,
        [jax.ShapeDtypeStruct((peers, 2 * tile, width), BF16)], [pltpu.HBM],
        [
            pltpu.VMEM(tiles.shape, BF16), pltpu.VMEM(nodes.shape, BF16), pltpu.VMEM(grads.shape, BF16),
            pltpu.VMEM((peers, tile, width), BF16), pltpu.SemaphoreType.DMA((2,)), pltpu.SemaphoreType.DMA((peers // group,)),
            pltpu.SemaphoreType.DMA((peers,)), pltpu.SemaphoreType.DMA((peers,)),
        ],
        flops=2 * peers * tile * tile * width, name="prepare", vmem=VMEM_MOST,
    )[0]


def local_both(sources, targets, tiles, nodes, grads):
    many, tile, _ = tiles.shape
    group = group_of(many)

    def body(src_ref, dst_ref, tiles_ref, nodes_ref, grads_ref, fwd_ref, bwd_ref):
        step = pl.program_id(0)

        @pl.when(step == 0)
        def _():
            fwd_ref[...] = jnp.zeros_like(fwd_ref)
            bwd_ref[...] = jnp.zeros_like(bwd_ref)

        for j in range(group):
            src = src_ref[step * group + j]
            dst = dst_ref[step * group + j]
            fwd_ref[dst] += dot(tiles_ref[j], nodes_ref[src])
            bwd_ref[src] += dot_t(tiles_ref[j], grads_ref[dst])

    shape = jax.ShapeDtypeStruct(nodes.shape, F32)
    return call(
        body, (sources, targets), (tiles, nodes, grads), (many // group,),
        [lead((group, tile, tile)), whole(nodes.shape), whole(grads.shape)],
        [whole(nodes.shape)] * 2, [shape, shape],
        flops=4 * many * tile * tile * nodes.shape[2], name="local_both",
    )


def streamed(received, offset, tile, buffer, sems, group):
    def copy(g):
        part = pl.ds(g * group, group)
        return pltpu.make_async_copy(received.at[part, pl.ds(offset, tile)], buffer.at[part], sems.at[g])

    return copy


def remote_forward(targets, tiles, received, base, stream):
    peers, tile, _ = tiles.shape
    width = received.shape[2]
    group = 4 if peers % 4 == 0 else 1

    def body(dst_ref, tiles_ref, recv_hbm, base_ref, out_ref, acc_ref, *rest):
        if stream:
            recv_ref, sems = rest
            copy = streamed(recv_hbm, 0, tile, recv_ref, sems, group)
            each(peers // group, lambda g: copy(g).start())
        else:
            recv_ref = recv_hbm
        acc_ref[...] = base_ref[...]

        def work(g):
            if stream:
                copy(g).wait()
            for j in range(group):
                p = g * group + j
                acc_ref[dst_ref[p]] += dot(tiles_ref[p], recv_ref[p, :tile])

        each(peers // group, work)
        out_ref[...] = acc_ref[...].astype(BF16)

    scratch = [pltpu.VMEM(base.shape, F32)]
    if stream:
        scratch += [pltpu.VMEM((peers, tile, width), BF16), pltpu.SemaphoreType.DMA((peers // group,))]
    return direct(
        body, (targets,), [tiles, received, base], [pltpu.VMEM, pltpu.HBM if stream else pltpu.VMEM, pltpu.VMEM],
        [jax.ShapeDtypeStruct(base.shape, BF16)], [pltpu.VMEM], scratch,
        flops=2 * peers * tile * tile * width, name="remote_forward",
    )[0]


def layer_one(z_mine, z_other, w_in):
    half = z_mine.shape[1]
    pre = dot(z_mine, w_in[:half]) + dot(z_other, w_in[half:])
    return pre, 0.5 * jnp.tanh(0.5 * pre) + 0.5


def supplied_product(zm_ref, zo_ref, wi_ref, wo_ref, prod_ref):
    count, tile, half = prod_ref.shape
    per = 2 if count % 2 == 0 else 1
    for r in range(count // per):
        part = slice(r * per * tile, (r + 1) * per * tile)
        pre, s = layer_one(zm_ref[part], zo_ref[part], wi_ref)
        prod = dot((pre * s).astype(BF16), wo_ref[:, :half]).astype(BF16)
        prod_ref[r * per : (r + 1) * per] = prod.reshape(per, tile, half)


def middle(ids, flags, z_mine, z_other, w_in, w_out, hist_out):
    rows, half = z_mine.shape
    peers = ids.shape[0]
    count, tile, _ = hist_out.shape
    group = group_of(peers)

    def body(ids_ref, flag_ref, zm_ref, zo_ref, wi_ref, wo_ref, hw_ref, send_hbm, prod_ref, sems):
        def supply(source, p):
            return pltpu.make_async_copy(source.at[ids_ref[p]], send_hbm.at[p], sems.at[p])

        def stored(g):
            for j in range(group):
                p = g * group + j
                pl.when(flag_ref[p] != 1)(lambda: supply(hw_ref, p).start())

        def fresh(g):
            for j in range(group):
                p = g * group + j
                pl.when(flag_ref[p] == 1)(lambda: supply(prod_ref, p).start())

        def finish(g):
            for j in range(group):
                supply(hw_ref, g * group + j).wait()

        each(peers // group, stored)
        supplied_product(zm_ref, zo_ref, wi_ref, wo_ref, prod_ref)
        each(peers // group, fresh)
        each(peers // group, finish)

    return direct(
        body, (ids, flags), [z_mine, z_other, w_in, w_out, hist_out], [pltpu.VMEM] * 5,
        [jax.ShapeDtypeStruct((peers, tile, half), BF16)], [pltpu.HBM],
        [pltpu.VMEM(hist_out.shape, BF16), pltpu.SemaphoreType.DMA((peers,))],
        flops=120 * rows * half * half, name="middle", vmem=61 * 1024 * 1024,
    )[0]


def local_out(sources, targets, tiles, sums_mine, sums_other, w_in, w_out):
    many, tile, _ = tiles.shape
    _, rows, half = sums_mine.shape
    shape = (rows // tile, tile, half)

    def body(src_ref, dst_ref, tiles_ref, sm_hbm, so_hbm, wi_ref, wo_ref, out_ref, zm_ref, zo_ref, prod_ref, sems):
        copies = [
            pltpu.make_async_copy(sm_hbm.at[2], zm_ref, sems.at[0]),
            pltpu.make_async_copy(so_hbm.at[2], zo_ref, sems.at[1]),
        ]
        for copy in copies:
            copy.start()
        for copy in copies:
            copy.wait()
        supplied_product(zm_ref, zo_ref, wi_ref, wo_ref, prod_ref)
        out_ref[...] = jnp.zeros_like(out_ref)
        for k in range(many):
            out_ref[dst_ref[k]] += dot(tiles_ref[k], prod_ref[src_ref[k]])

    return direct(
        body, (sources, targets), [tiles, sums_mine, sums_other, w_in, w_out],
        [pltpu.VMEM] + [pltpu.HBM] * 2 + [pltpu.VMEM] * 2,
        [jax.ShapeDtypeStruct(shape, F32)], [pltpu.VMEM],
        [
            pltpu.VMEM((rows, half), BF16), pltpu.VMEM((rows, half), BF16), pltpu.VMEM(shape, BF16),
            pltpu.SemaphoreType.DMA((2,)),
        ],
        flops=12 * rows * half * half + 2 * many * tile * tile * half, name="local_out",
    )[0]


def gather_grads(ids, flags, returned, base, z_mine):
    peers = returned.shape[0]
    count, tile, width = base.shape
    group = 4 if peers % 4 == 0 else 1
    both = (2,) + base.shape

    def body(ids_ref, flag_ref, ret_ref, base_ref, z_ref, out_ref, acc_ref):
        out_ref[2] = z_ref[...]
        acc_ref[0] = base_ref[...]
        acc_ref[1] = jnp.zeros_like(base_ref)

        def work(g):
            for j in range(group):
                p = g * group + j
                side = jnp.where(flag_ref[p] == 1, 0, 1)
                acc_ref[side, ids_ref[p]] += ret_ref[p, tile:].astype(F32)

        each(peers // group, work)
        out_ref[:2] = acc_ref[...].astype(BF16)

    return direct(
        body, (ids, flags), [returned, base, z_mine], [pltpu.VMEM] * 3,
        [jax.ShapeDtypeStruct((3,) + base.shape, BF16)], [pltpu.VMEM], [pltpu.VMEM(both, F32)],
        flops=32 * peers * tile * tile * width, name="gather_grads",
    )[0]


def chunking(peers, total, width):
    row_chunks = min(peers, total // 16)
    col_chunks = peers // row_chunks
    return row_chunks, col_chunks, total // row_chunks, width // col_chunks


def backward(place, sums_mine, sums_other, history, w_in, w_out, peers):
    _, rows, half = sums_mine.shape
    row_chunks, col_chunks, chunk_rows, chunk_cols = chunking(peers, 2 * half, 2 * half)
    parts = 2
    span = rows // parts

    def body(place_ref, sm_hbm, so_hbm, hist_ref, wi_ref, wo_ref, gh_hbm, chunk_ref, sm_ref, so_ref, gh_ref, acc_ref, sm_sem, so_sem, gh_sem):
        me, side = place_ref[0], place_ref[1]
        own = pl.ds(pl.multiple_of(side * half, half), half)
        far = pl.ds(pl.multiple_of((1 - side) * half, half), half)

        def sums_in(r):
            part = pl.ds(r * span, span)
            return (
                pltpu.make_async_copy(sm_hbm.at[:, part], sm_ref.at[:, part], sm_sem.at[r]),
                pltpu.make_async_copy(so_hbm.at[:, part], so_ref.at[:, part], so_sem.at[r]),
            )

        def gh_out(r):
            part = pl.ds(r * span, span)
            return pltpu.make_async_copy(gh_ref.at[part], gh_hbm.at[part], gh_sem.at[r])

        for r in range(parts):
            for copy in sums_in(r):
                copy.start()
        for r in range(parts):
            part = slice(r * span, (r + 1) * span)

            def add(rows_, cols, value):
                if r == 0:
                    acc_ref[rows_, cols] = value
                else:
                    acc_ref[rows_, cols] += value

            for copy in sums_in(r):
                copy.wait()
            z, hist = sm_ref[2, part], hist_ref[part]
            pre, s = layer_one(z, so_ref[2, part], wi_ref)
            hid = (pre[:, :half] * s[:, :half]).astype(BF16)
            dh = dot_nt(sm_ref[0, part], wo_ref[:, :half]) + dot_nt(so_ref[0, part], wo_ref[:, half:])
            gh_ref[part] = dh[:, :half].astype(BF16)
            gh_out(r).start()
            dpre = (dh * s * (1.0 + pre * (1.0 - s))).astype(BF16)
            add(slice(0, half), own, dot_t(z, dpre[:, :half]))
            add(slice(0, half), far, dot_t(z, dpre[:, half:]))
            add(slice(half, 2 * half), own, dot_t(hid, sm_ref[0, part]) + dot_t(hist, sm_ref[1, part]))
            add(slice(half, 2 * half), far, dot_t(hid, so_ref[0, part]) + dot_t(hist, so_ref[1, part]))
        for c in range(peers):
            r, k = c // col_chunks, c % col_chunks
            piece = acc_ref[r * chunk_rows : (r + 1) * chunk_rows, k * chunk_cols : (k + 1) * chunk_cols]
            chunk_ref[c ^ me] = piece.astype(BF16)
        for r in range(parts):
            gh_out(r).wait()

    return direct(
        body, (place,), [sums_mine, sums_other, history, w_in, w_out],
        [pltpu.HBM] * 2 + [pltpu.VMEM] * 3,
        [
            jax.ShapeDtypeStruct((rows, half), BF16),
            jax.ShapeDtypeStruct((peers, chunk_rows, chunk_cols), BF16),
        ],
        [pltpu.HBM, pltpu.VMEM],
        [
            pltpu.VMEM((3, rows, half), BF16), pltpu.VMEM((3, rows, half), BF16),
            pltpu.VMEM((rows, half), BF16), pltpu.VMEM((2 * half, 2 * half), F32),
            pltpu.SemaphoreType.DMA((parts,)), pltpu.SemaphoreType.DMA((parts,)), pltpu.SemaphoreType.DMA((parts,)),
        ],
        flops=28 * rows * half * half, name="backward",
    )


def finish_weights(place, chunks, half, scale):
    peers, chunk_rows, chunk_cols = chunks.shape
    _, col_chunks, _, _ = chunking(peers, 2 * half, 2 * half)
    steps = 4
    span = half // steps

    def body(place_ref, chunk_ref, in_hbm, out_hbm, all_ref, sems):
        def leave(k):
            target = in_hbm if k < steps else out_hbm
            return pltpu.make_async_copy(
                all_ref.at[pl.ds(k * span, span)], target.at[pl.ds(k % steps * span, span)], sems.at[k]
            )

        me = place_ref[0]
        sent = 0
        for c in range(peers):
            r, k = (c // col_chunks) * chunk_rows, c % col_chunks
            piece = chunk_ref[c ^ me].astype(F32) * scale
            all_ref[r : r + chunk_rows, k * chunk_cols : (k + 1) * chunk_cols] = piece
            if k == col_chunks - 1 and (r + chunk_rows) % span == 0:
                leave(sent).start()
                sent += 1
        for k in range(2 * steps):
            leave(k).wait()

    shape = jax.ShapeDtypeStruct((half, 2 * half), F32)
    return direct(
        body, (place,), [chunks], [pltpu.VMEM], [shape, shape], [pltpu.HBM] * 2,
        [pltpu.VMEM((2 * half, 2 * half), F32), pltpu.SemaphoreType.DMA((2 * steps,))], name="finish_weights",
    )


def digit(peers):
    return min(4, peers)


def hop(value, peers, offset):
    return lax.ppermute(value, "dom", [(i, i ^ offset) for i in range(peers)])


def scatter_digit(chunks, peers):
    radix = digit(peers)
    parts = chunks.reshape((-1, radix) + chunks.shape[1:])
    return parts[:, 0], [hop(parts[:, t], peers, t) for t in range(1, radix)]


def add_pieces(kept, arrived):
    total = kept.astype(F32)
    for piece in arrived:
        total = total + piece.astype(F32)
    return total.astype(BF16)


def gather_digit(held, peers):
    arrived = [held] + [hop(held, peers, t) for t in range(1, digit(peers))]
    return jnp.stack(arrived, axis=1).reshape((-1,) + held.shape[1:])


def tie(values):
    return lax.optimization_barrier(values)


def exchange(sending):
    return lax.all_to_all(sending, "dom", split_axis=0, concat_axis=0, tiled=True)


def swap(value):
    return lax.ppermute(value, "hid", SWAP)


def per_device(
    features,
    history,
    remote_tiles,
    remote_dst,
    serve_block,
    push_flag,
    local_tiles,
    local_src,
    local_dst,
    weight_in,
    weight_out,
    cotangent,
):
    tile = remote_tiles.shape[-1]
    rows, half = features.shape
    count = rows // tile
    peers = remote_tiles.shape[1]
    tiles_remote, tiles_local = remote_tiles[0], local_tiles[0]
    targets_remote, served_ids, flags = remote_dst[0], serve_block[0], push_flag[0]
    sources_local, targets_local = local_src[0], local_dst[0]
    side = lax.axis_index("hid")
    place = jnp.stack([lax.axis_index("dom") % digit(peers), side]).astype(jnp.int32)

    def blocks(values):
        return values.reshape(count, tile, half)

    def own_first(weight):
        joined = jnp.concatenate([weight, swap(weight)], axis=0)
        turned = jnp.concatenate([joined[:, half:], joined[:, :half]], axis=1)
        return jnp.where(side == 0, joined, turned)

    feat_blocks, grad_blocks = blocks(features), blocks(cotangent)
    first = prepare(served_ids, targets_remote, tiles_remote, feat_blocks, grad_blocks)
    received = exchange(first)
    base_forward, base_back = local_both(sources_local, targets_local, tiles_local, feat_blocks, grad_blocks)
    w_in, w_out = own_first(weight_in), own_first(weight_out)
    hist_out = dot(history, w_out[:half, :half]) + dot(swap(history), w_out[half:, :half])
    hist_out = blocks(hist_out.astype(BF16))

    received, w_in, w_out, hist_out, base_forward, base_back = tie(
        (received, w_in, w_out, hist_out, base_forward, base_back)
    )
    z_first = remote_forward(targets_remote, tiles_remote, received, base_forward, False).reshape(rows, half)
    z_first, received = tie((z_first, received))
    z_other = swap(z_first)
    sums = gather_grads(served_ids, flags, received, base_back, blocks(z_first)).reshape(3, rows, half)
    sums_other = swap(sums)
    sending = middle(served_ids, flags, z_first, z_other, w_in, w_out, hist_out)
    sending, sums = tie((sending, sums))
    supplied = exchange(sending)
    grad_hidden, chunks = backward(
        place, sums, sums_other, history, w_in, w_out, peers
    )
    kept, arrived = scatter_digit(chunks, peers)
    kept, sums = tie((kept, sums))
    base_out = local_out(sources_local, targets_local, tiles_local, sums, sums_other, w_in, w_out)
    kept, base_out = tie((kept, base_out))
    held = add_pieces(kept, arrived)
    offset = digit(peers)
    while offset < peers:
        held = add_pieces(held, [hop(held, peers, offset)])
        offset *= 2
    held, supplied = tie((held, supplied))
    held = gather_digit(held, peers)
    out = remote_forward(targets_remote, tiles_remote, supplied, base_out, True)
    held, out = tie((held, out))
    scale = float(rows * peers) ** (-0.5)
    grad_in, grad_out = finish_weights(place, held, half, scale)
    out = out.reshape(rows, half)
    return (out, grad_hidden, grad_in, grad_out)


def solution(mesh):
    return jax.shard_map(
        per_device,
        mesh=mesh,
        in_specs=(
            P("dom", "hid"),
            P("dom", "hid"),
            P("dom", None, None, None),
            P("dom", None),
            P("dom", None),
            P("dom", None),
            P("dom", None, None, None),
            P("dom", None),
            P("dom", None),
            P("hid", None),
            P("hid", None),
            P("dom", "hid"),
        ),
        out_specs=(P("dom", "hid"), P("dom", "hid"), P("hid", None), P("hid", None)),
        check_vma=False,
    )
```

```python
import math

import jax
import jax.numpy as jnp
from jax import lax
from jax.experimental import pallas as pl
from jax.experimental.pallas import tpu as pltpu
from jax.sharding import PartitionSpec as P

BF16 = jnp.bfloat16
F32 = jnp.float32
VMEM_SPARE = 6 * 1024 * 1024
VMEM_MOST = 60 * 1024 * 1024
SWAP = ((0, 1), (1, 0))


def dot(a, b):
    return jnp.dot(a, b, preferred_element_type=F32)


def dot_t(a, b):
    return lax.dot_general(a, b, (((0,), (0,)), ((), ())), preferred_element_type=F32)


def dot_nt(a, b):
    return lax.dot_general(a, b, (((1,), (1,)), ((), ())), preferred_element_type=F32)


def call(body, scalars, arrays, grid, in_specs, out_specs, out_shape, scratch=(), flops=0, name=None, vmem=None):
    if vmem is None:
        vmem = VMEM_SPARE + 2 * sum(math.prod(spec.block_shape) * a.dtype.itemsize for spec, a in zip(in_specs, arrays))
        vmem += 2 * sum(
            math.prod(spec.block_shape) * s.dtype.itemsize
            for spec, s in zip(jax.tree.leaves(out_specs), jax.tree.leaves(out_shape))
        )
        vmem += sum(math.prod(s.shape) * jnp.dtype(s.dtype).itemsize for s in scratch)
    moved = sum(a.size * a.dtype.itemsize for a in arrays)
    moved += sum(s.size * s.dtype.itemsize for s in jax.tree.leaves(out_shape))
    return pl.pallas_call(
        body,
        grid_spec=pltpu.PrefetchScalarGridSpec(
            num_scalar_prefetch=len(scalars),
            grid=grid,
            in_specs=in_specs,
            out_specs=out_specs,
            scratch_shapes=list(scratch),
        ),
        out_shape=out_shape,
        compiler_params=pltpu.CompilerParams(vmem_limit_bytes=vmem),
        cost_estimate=pl.CostEstimate(flops=int(flops), bytes_accessed=int(moved), transcendentals=0),
        name=name,
    )(*scalars, *arrays)


def direct(body, scalars, arrays, in_spaces, out_shape, out_spaces, scratch=(), flops=0, name=None, vmem=None):
    inside = [a for a, space in zip(arrays + out_shape, in_spaces + out_spaces) if space is pltpu.VMEM]
    sizes = [math.prod(a.shape) * jnp.dtype(a.dtype).itemsize for a in inside]
    sizes += [math.prod(a.shape) * jnp.dtype(a.dtype).itemsize for a in scratch if getattr(a, "memory_space", None) is pltpu.VMEM]
    moved = sum(math.prod(a.shape) * jnp.dtype(a.dtype).itemsize for a in arrays + out_shape)
    return pl.pallas_call(
        body,
        in_specs=[pl.BlockSpec(memory_space=pltpu.SMEM)] * len(scalars)
        + [pl.BlockSpec(memory_space=space) for space in in_spaces],
        out_specs=[pl.BlockSpec(memory_space=space) for space in out_spaces],
        out_shape=out_shape,
        scratch_shapes=list(scratch),
        compiler_params=pltpu.CompilerParams(vmem_limit_bytes=vmem or sum(sizes) + VMEM_SPARE),
        cost_estimate=pl.CostEstimate(flops=int(flops), bytes_accessed=int(moved), transcendentals=0),
        name=name,
    )(*scalars, *arrays)


def each(count, step):
    if count <= 4:
        for i in range(count):
            step(i)
    else:
        pl.loop(0, count)(step)


def whole(shape):
    return pl.BlockSpec(shape, lambda i, *_: (0,) * len(shape))


def lead(shape):
    return pl.BlockSpec(shape, lambda i, *_: (i,) + (0,) * (len(shape) - 1))


def group_of(peers):
    return 8 if peers % 8 == 0 else 1


def prepare(ids, targets, tiles, nodes, grads):
    peers, tile, _ = tiles.shape
    width = nodes.shape[2]
    group = group_of(peers)

    def body(ids_ref, dst_ref, tiles_hbm, nodes_hbm, grads_hbm, out_hbm, tiles_ref, nodes_ref, grads_ref, back_ref, in_sem, tile_sem, pick_sem, out_sem):
        def tiles_in(g):
            part = pl.ds(g * group, group)
            return pltpu.make_async_copy(tiles_hbm.at[part], tiles_ref.at[part], tile_sem.at[g])

        def pick(p):
            return pltpu.make_async_copy(nodes_ref.at[ids_ref[p]], out_hbm.at[p, pl.ds(0, tile)], pick_sem.at[p])

        def give(p):
            return pltpu.make_async_copy(back_ref.at[p], out_hbm.at[p, pl.ds(tile, tile)], out_sem.at[p])

        def picks(g):
            for j in range(group):
                pick(g * group + j).start()

        nodes_in = pltpu.make_async_copy(nodes_hbm, nodes_ref, in_sem.at[0])
        grads_in = pltpu.make_async_copy(grads_hbm, grads_ref, in_sem.at[1])
        nodes_in.start()
        grads_in.start()
        each(peers // group, lambda g: tiles_in(g).start())
        nodes_in.wait()
        each(peers // group, picks)
        grads_in.wait()

        def work(g):
            tiles_in(g).wait()
            for j in range(group):
                p = g * group + j
                back_ref[p] = dot_t(tiles_ref[p], grads_ref[dst_ref[p]]).astype(BF16)
                give(p).start()

        def finish(g):
            for j in range(group):
                give(g * group + j).wait()
                pick(g * group + j).wait()

        each(peers // group, work)
        each(peers // group, finish)

    return direct(
        body, (ids, targets), [tiles, nodes, grads], [pltpu.HBM] * 3,
        [jax.ShapeDtypeStruct((peers, 2 * tile, width), BF16)], [pltpu.HBM],
        [
            pltpu.VMEM(tiles.shape, BF16), pltpu.VMEM(nodes.shape, BF16), pltpu.VMEM(grads.shape, BF16),
            pltpu.VMEM((peers, tile, width), BF16), pltpu.SemaphoreType.DMA((2,)), pltpu.SemaphoreType.DMA((peers // group,)),
            pltpu.SemaphoreType.DMA((peers,)), pltpu.SemaphoreType.DMA((peers,)),
        ],
        flops=2 * peers * tile * tile * width, name="prepare", vmem=VMEM_MOST,
    )[0]


def local_both(sources, targets, tiles, nodes, grads):
    many, tile, _ = tiles.shape
    group = group_of(many)

    def body(src_ref, dst_ref, tiles_ref, nodes_ref, grads_ref, fwd_ref, bwd_ref):
        step = pl.program_id(0)

        @pl.when(step == 0)
        def _():
            fwd_ref[...] = jnp.zeros_like(fwd_ref)
            bwd_ref[...] = jnp.zeros_like(bwd_ref)

        for j in range(group):
            src = src_ref[step * group + j]
            dst = dst_ref[step * group + j]
            fwd_ref[dst] += dot(tiles_ref[j], nodes_ref[src])
            bwd_ref[src] += dot_t(tiles_ref[j], grads_ref[dst])

    shape = jax.ShapeDtypeStruct(nodes.shape, F32)
    return call(
        body, (sources, targets), (tiles, nodes, grads), (many // group,),
        [lead((group, tile, tile)), whole(nodes.shape), whole(grads.shape)],
        [whole(nodes.shape)] * 2, [shape, shape],
        flops=4 * many * tile * tile * nodes.shape[2], name="local_both",
    )


def streamed(received, offset, tile, buffer, sems, group):
    def copy(g):
        part = pl.ds(g * group, group)
        return pltpu.make_async_copy(received.at[part, pl.ds(offset, tile)], buffer.at[part], sems.at[g])

    return copy


def remote_forward(targets, tiles, received, base, stream):
    peers, tile, _ = tiles.shape
    width = received.shape[2]
    group = 4 if peers % 4 == 0 else 1

    def body(dst_ref, tiles_ref, recv_hbm, base_ref, out_ref, acc_ref, *rest):
        if stream:
            recv_ref, sems = rest
            copy = streamed(recv_hbm, 0, tile, recv_ref, sems, group)
            each(peers // group, lambda g: copy(g).start())
        else:
            recv_ref = recv_hbm
        acc_ref[...] = base_ref[...]

        def work(g):
            if stream:
                copy(g).wait()
            for j in range(group):
                p = g * group + j
                acc_ref[dst_ref[p]] += dot(tiles_ref[p], recv_ref[p, :tile])

        each(peers // group, work)
        out_ref[...] = acc_ref[...].astype(BF16)

    scratch = [pltpu.VMEM(base.shape, F32)]
    if stream:
        scratch += [pltpu.VMEM((peers, tile, width), BF16), pltpu.SemaphoreType.DMA((peers // group,))]
    return direct(
        body, (targets,), [tiles, received, base], [pltpu.VMEM, pltpu.HBM if stream else pltpu.VMEM, pltpu.VMEM],
        [jax.ShapeDtypeStruct(base.shape, BF16)], [pltpu.VMEM], scratch,
        flops=2 * peers * tile * tile * width, name="remote_forward",
    )[0]


def layer_one(z_mine, z_other, w_in):
    half = z_mine.shape[1]
    pre = dot(z_mine, w_in[:half]) + dot(z_other, w_in[half:])
    return pre, 0.5 * jnp.tanh(0.5 * pre) + 0.5


def supplied_product(zm_ref, zo_ref, wi_ref, wo_ref, prod_ref):
    count, tile, half = prod_ref.shape
    per = 2 if count % 2 == 0 else 1
    for r in range(count // per):
        part = slice(r * per * tile, (r + 1) * per * tile)
        pre, s = layer_one(zm_ref[part], zo_ref[part], wi_ref)
        prod = dot((pre * s).astype(BF16), wo_ref[:, :half]).astype(BF16)
        prod_ref[r * per : (r + 1) * per] = prod.reshape(per, tile, half)


def middle(ids, flags, z_mine, z_other, w_in, w_out, hist_out):
    rows, half = z_mine.shape
    peers = ids.shape[0]
    count, tile, _ = hist_out.shape
    group = group_of(peers)

    def body(ids_ref, flag_ref, zm_ref, zo_ref, wi_ref, wo_ref, hw_ref, send_hbm, prod_ref, sems):
        def supply(source, p):
            return pltpu.make_async_copy(source.at[ids_ref[p]], send_hbm.at[p], sems.at[p])

        def stored(g):
            for j in range(group):
                p = g * group + j
                pl.when(flag_ref[p] != 1)(lambda: supply(hw_ref, p).start())

        def fresh(g):
            for j in range(group):
                p = g * group + j
                pl.when(flag_ref[p] == 1)(lambda: supply(prod_ref, p).start())

        def finish(g):
            for j in range(group):
                supply(hw_ref, g * group + j).wait()

        each(peers // group, stored)
        supplied_product(zm_ref, zo_ref, wi_ref, wo_ref, prod_ref)
        each(peers // group, fresh)
        each(peers // group, finish)

    return direct(
        body, (ids, flags), [z_mine, z_other, w_in, w_out, hist_out], [pltpu.VMEM] * 5,
        [jax.ShapeDtypeStruct((peers, tile, half), BF16)], [pltpu.HBM],
        [pltpu.VMEM(hist_out.shape, BF16), pltpu.SemaphoreType.DMA((peers,))],
        flops=120 * rows * half * half, name="middle", vmem=61 * 1024 * 1024,
    )[0]


def local_out(sources, targets, tiles, sums_mine, sums_other, w_in, w_out):
    many, tile, _ = tiles.shape
    _, rows, half = sums_mine.shape
    shape = (rows // tile, tile, half)

    def body(src_ref, dst_ref, tiles_ref, sm_hbm, so_hbm, wi_ref, wo_ref, out_ref, zm_ref, zo_ref, prod_ref, sems):
        copies = [
            pltpu.make_async_copy(sm_hbm.at[2], zm_ref, sems.at[0]),
            pltpu.make_async_copy(so_hbm.at[2], zo_ref, sems.at[1]),
        ]
        for copy in copies:
            copy.start()
        for copy in copies:
            copy.wait()
        supplied_product(zm_ref, zo_ref, wi_ref, wo_ref, prod_ref)
        out_ref[...] = jnp.zeros_like(out_ref)
        for k in range(many):
            out_ref[dst_ref[k]] += dot(tiles_ref[k], prod_ref[src_ref[k]])

    return direct(
        body, (sources, targets), [tiles, sums_mine, sums_other, w_in, w_out],
        [pltpu.VMEM] + [pltpu.HBM] * 2 + [pltpu.VMEM] * 2,
        [jax.ShapeDtypeStruct(shape, F32)], [pltpu.VMEM],
        [
            pltpu.VMEM((rows, half), BF16), pltpu.VMEM((rows, half), BF16), pltpu.VMEM(shape, BF16),
            pltpu.SemaphoreType.DMA((2,)),
        ],
        flops=12 * rows * half * half + 2 * many * tile * tile * half, name="local_out",
    )[0]


def gather_grads(ids, flags, returned, base, z_mine):
    peers = returned.shape[0]
    count, tile, width = base.shape
    group = 4 if peers % 4 == 0 else 1
    both = (2,) + base.shape

    def body(ids_ref, flag_ref, ret_ref, base_ref, z_ref, out_ref, acc_ref):
        out_ref[2] = z_ref[...]
        acc_ref[0] = base_ref[...]
        acc_ref[1] = jnp.zeros_like(base_ref)

        def work(g):
            for j in range(group):
                p = g * group + j
                side = jnp.where(flag_ref[p] == 1, 0, 1)
                acc_ref[side, ids_ref[p]] += ret_ref[p, tile:].astype(F32)

        each(peers // group, work)
        out_ref[:2] = acc_ref[...].astype(BF16)

    return direct(
        body, (ids, flags), [returned, base, z_mine], [pltpu.VMEM] * 3,
        [jax.ShapeDtypeStruct((3,) + base.shape, BF16)], [pltpu.VMEM], [pltpu.VMEM(both, F32)],
        flops=32 * peers * tile * tile * width, name="gather_grads",
    )[0]


def chunking(peers, total, width):
    row_chunks = min(peers, total // 16)
    col_chunks = peers // row_chunks
    return row_chunks, col_chunks, total // row_chunks, width // col_chunks


def backward(place, sums_mine, sums_other, history, w_in, w_out, peers):
    _, rows, half = sums_mine.shape
    row_chunks, col_chunks, chunk_rows, chunk_cols = chunking(peers, 2 * half, 2 * half)
    parts = 2
    span = rows // parts

    def body(place_ref, sm_hbm, so_hbm, hist_ref, wi_ref, wo_ref, gh_hbm, chunk_ref, sm_ref, so_ref, gh_ref, acc_ref, sm_sem, so_sem, gh_sem):
        me, side = place_ref[0], place_ref[1]
        own = pl.ds(pl.multiple_of(side * half, half), half)
        far = pl.ds(pl.multiple_of((1 - side) * half, half), half)

        def sums_in(r):
            part = pl.ds(r * span, span)
            return (
                pltpu.make_async_copy(sm_hbm.at[:, part], sm_ref.at[:, part], sm_sem.at[r]),
                pltpu.make_async_copy(so_hbm.at[:, part], so_ref.at[:, part], so_sem.at[r]),
            )

        def gh_out(r):
            part = pl.ds(r * span, span)
            return pltpu.make_async_copy(gh_ref.at[part], gh_hbm.at[part], gh_sem.at[r])

        for r in range(parts):
            for copy in sums_in(r):
                copy.start()
        for r in range(parts):
            part = slice(r * span, (r + 1) * span)

            def add(rows_, cols, value):
                if r == 0:
                    acc_ref[rows_, cols] = value
                else:
                    acc_ref[rows_, cols] += value

            for copy in sums_in(r):
                copy.wait()
            z, hist = sm_ref[2, part], hist_ref[part]
            pre, s = layer_one(z, so_ref[2, part], wi_ref)
            hid = (pre[:, :half] * s[:, :half]).astype(BF16)
            dh = dot_nt(sm_ref[0, part], wo_ref[:, :half]) + dot_nt(so_ref[0, part], wo_ref[:, half:])
            gh_ref[part] = dh[:, :half].astype(BF16)
            gh_out(r).start()
            dpre = (dh * s * (1.0 + pre * (1.0 - s))).astype(BF16)
            add(slice(0, half), own, dot_t(z, dpre[:, :half]))
            add(slice(0, half), far, dot_t(z, dpre[:, half:]))
            add(slice(half, 2 * half), own, dot_t(hid, sm_ref[0, part]) + dot_t(hist, sm_ref[1, part]))
            add(slice(half, 2 * half), far, dot_t(hid, so_ref[0, part]) + dot_t(hist, so_ref[1, part]))
        for c in range(peers):
            r, k = c // col_chunks, c % col_chunks
            piece = acc_ref[r * chunk_rows : (r + 1) * chunk_rows, k * chunk_cols : (k + 1) * chunk_cols]
            chunk_ref[c ^ me] = piece.astype(BF16)
        for r in range(parts):
            gh_out(r).wait()

    return direct(
        body, (place,), [sums_mine, sums_other, history, w_in, w_out],
        [pltpu.HBM] * 2 + [pltpu.VMEM] * 3,
        [
            jax.ShapeDtypeStruct((rows, half), BF16),
            jax.ShapeDtypeStruct((peers, chunk_rows, chunk_cols), BF16),
        ],
        [pltpu.HBM, pltpu.VMEM],
        [
            pltpu.VMEM((3, rows, half), BF16), pltpu.VMEM((3, rows, half), BF16),
            pltpu.VMEM((rows, half), BF16), pltpu.VMEM((2 * half, 2 * half), F32),
            pltpu.SemaphoreType.DMA((parts,)), pltpu.SemaphoreType.DMA((parts,)), pltpu.SemaphoreType.DMA((parts,)),
        ],
        flops=28 * rows * half * half, name="backward",
    )


def finish_weights(place, chunks, half, scale):
    peers, chunk_rows, chunk_cols = chunks.shape
    _, col_chunks, _, _ = chunking(peers, 2 * half, 2 * half)
    steps = 4
    span = half // steps

    def body(place_ref, chunk_ref, in_hbm, out_hbm, all_ref, sems):
        def leave(k):
            target = in_hbm if k < steps else out_hbm
            return pltpu.make_async_copy(
                all_ref.at[pl.ds(k * span, span)], target.at[pl.ds(k % steps * span, span)], sems.at[k]
            )

        me = place_ref[0]
        sent = 0
        for c in range(peers):
            r, k = (c // col_chunks) * chunk_rows, c % col_chunks
            piece = chunk_ref[c ^ me].astype(F32) * scale
            all_ref[r : r + chunk_rows, k * chunk_cols : (k + 1) * chunk_cols] = piece
            if k == col_chunks - 1 and (r + chunk_rows) % span == 0:
                leave(sent).start()
                sent += 1
        for k in range(2 * steps):
            leave(k).wait()

    shape = jax.ShapeDtypeStruct((half, 2 * half), F32)
    return direct(
        body, (place,), [chunks], [pltpu.VMEM], [shape, shape], [pltpu.HBM] * 2,
        [pltpu.VMEM((2 * half, 2 * half), F32), pltpu.SemaphoreType.DMA((2 * steps,))], name="finish_weights",
    )


def digit(peers):
    return min(4, peers)


def hop(value, peers, offset):
    return lax.ppermute(value, "dom", [(i, i ^ offset) for i in range(peers)])


def scatter_digit(chunks, peers):
    radix = digit(peers)
    parts = chunks.reshape((-1, radix) + chunks.shape[1:])
    return parts[:, 0], [hop(parts[:, t], peers, t) for t in reversed(range(1, radix))]


def add_pieces(kept, arrived):
    total = kept.astype(F32)
    for piece in arrived:
        total = total + piece.astype(F32)
    return total.astype(BF16)


def gather_digit(held, peers):
    arrived = [held] + [hop(held, peers, t) for t in range(1, digit(peers))]
    return jnp.stack(arrived, axis=1).reshape((-1,) + held.shape[1:])


def tie(values):
    return lax.optimization_barrier(values)


def exchange(sending):
    return lax.all_to_all(sending, "dom", split_axis=0, concat_axis=0, tiled=True)


def swap(value):
    return lax.ppermute(value, "hid", SWAP)


def per_device(
    features,
    history,
    remote_tiles,
    remote_dst,
    serve_block,
    push_flag,
    local_tiles,
    local_src,
    local_dst,
    weight_in,
    weight_out,
    cotangent,
):
    tile = remote_tiles.shape[-1]
    rows, half = features.shape
    count = rows // tile
    peers = remote_tiles.shape[1]
    tiles_remote, tiles_local = remote_tiles[0], local_tiles[0]
    targets_remote, served_ids, flags = remote_dst[0], serve_block[0], push_flag[0]
    sources_local, targets_local = local_src[0], local_dst[0]
    side = lax.axis_index("hid")
    place = jnp.stack([lax.axis_index("dom") % digit(peers), side]).astype(jnp.int32)

    def blocks(values):
        return values.reshape(count, tile, half)

    def own_first(weight):
        joined = jnp.concatenate([weight, swap(weight)], axis=0)
        turned = jnp.concatenate([joined[:, half:], joined[:, :half]], axis=1)
        return jnp.where(side == 0, joined, turned)

    feat_blocks, grad_blocks = blocks(features), blocks(cotangent)
    first = prepare(served_ids, targets_remote, tiles_remote, feat_blocks, grad_blocks)
    received = exchange(first)
    base_forward, base_back = local_both(sources_local, targets_local, tiles_local, feat_blocks, grad_blocks)
    w_in, w_out = own_first(weight_in), own_first(weight_out)
    hist_out = dot(history, w_out[:half, :half]) + dot(swap(history), w_out[half:, :half])
    hist_out = blocks(hist_out.astype(BF16))

    received, w_in, w_out, hist_out, base_forward, base_back = tie(
        (received, w_in, w_out, hist_out, base_forward, base_back)
    )
    z_first = remote_forward(targets_remote, tiles_remote, received, base_forward, False).reshape(rows, half)
    z_first, received = tie((z_first, received))
    z_other = swap(z_first)
    sums = gather_grads(served_ids, flags, received, base_back, blocks(z_first)).reshape(3, rows, half)
    sums_other = swap(sums)
    sending = middle(served_ids, flags, z_first, z_other, w_in, w_out, hist_out)
    sending, sums = tie((sending, sums))
    supplied = exchange(sending)
    grad_hidden, chunks = backward(
        place, sums, sums_other, history, w_in, w_out, peers
    )
    kept, arrived = scatter_digit(chunks, peers)
    kept, sums = tie((kept, sums))
    base_out = local_out(sources_local, targets_local, tiles_local, sums, sums_other, w_in, w_out)
    kept, base_out = tie((kept, base_out))
    held = add_pieces(kept, arrived)
    offset = digit(peers)
    while offset < peers:
        held = add_pieces(held, [hop(held, peers, offset)])
        offset *= 2
    held, supplied = tie((held, supplied))
    held = gather_digit(held, peers)
    out = remote_forward(targets_remote, tiles_remote, supplied, base_out, True)
    held, out = tie((held, out))
    scale = float(rows * peers) ** (-0.5)
    grad_in, grad_out = finish_weights(place, held, half, scale)
    out = out.reshape(rows, half)
    return (out, grad_hidden, grad_in, grad_out)


def solution(mesh):
    return jax.shard_map(
        per_device,
        mesh=mesh,
        in_specs=(
            P("dom", "hid"),
            P("dom", "hid"),
            P("dom", None, None, None),
            P("dom", None),
            P("dom", None),
            P("dom", None),
            P("dom", None, None, None),
            P("dom", None),
            P("dom", None),
            P("hid", None),
            P("hid", None),
            P("dom", "hid"),
        ),
        out_specs=(P("dom", "hid"), P("dom", "hid"), P("hid", None), P("hid", None)),
        check_vma=False,
    )
```
